256 devices in a mesh: ctx: 32 (over z, x), head: 4 (over y_hi, core), dp: 2 (over y_lo).
Axes of the slice: x: 4, y: 4 (y_hi: 2, y_lo: 2; y = y_hi * 2 + y_lo), z: 8, core: 2. Of those that a mesh axis runs over, the one named last changes fastest.
Arguments:
- queries: bfloat16 [8192, 32, 128], P(('dp', 'ctx'), 'head'), parts along dimension 0, may hold values from -6 to 6
- key_rows: bfloat16 [8192, 4, 128], P(('dp', 'ctx'), 'head'), parts along dimension 0, may hold values from -6 to 6
- value_rows: bfloat16 [8192, 4, 128], P(('dp', 'ctx'), 'head'), parts along dimension 0, may hold values from -6 to 6
- token_pos: int32 [8192], P(('dp', 'ctx')), parts along dimension 0, may hold values from 0 to 4095, as said below
- step_len: int32 [128], P('dp'), parts along dimension 0, may hold values from 1 to 512, 4096 in all
- label_count: int32 [128], P('dp'), parts along dimension 0, may hold values from 0 to 8
- out_grad: bfloat16 [8192, 32, 128], P(('dp', 'ctx'), 'head'), parts along dimension 0, may hold values from -8 to 8
- reward_weight: bfloat16 [32, 128], P('head'), may hold values from -1.25 to 1.25
Outputs:
- step_loss: float32 [128], P('dp'), parts along dimension 0
- d_query: bfloat16 [8192, 32, 128], P(('dp', 'ctx'), 'head'), parts along dimension 0
- d_key: bfloat16 [8192, 4, 128], P(('dp', 'ctx'), 'head'), parts along dimension 0
- d_value: bfloat16 [8192, 4, 128], P(('dp', 'ctx'), 'head'), parts along dimension 0
- d_reward: float32 [64, 128], P(('dp', 'head')), parts along dimension 0
The draws below stay inside these ranges and needn't reach their ends.
There are 2 independent parts, one for each index of `dp`. The reference program is written for one: setup_inputs(seed, part) draws one part's arguments, and reference() takes and returns one part's arrays. A program takes and returns all parts, laid end to end along the dimension named above; an argument that names none is the same for every part. Nothing has to cross between parts.
Inputs may be any that keep to these rules, and one draw needn't show every extreme that they name: Each device's 128 rows of token_pos are two runs of 64 consecutive increasing positions, one beginning at c * 64 and the other at (63 - c) * 64 for a c of that device's own, in either order; over all 4096 rows every position appears once.
All inputs are finite; a program needn't handle non-finite values.
Results may differ from the reference program's by a relative error of at most 0.03.
Values may be sent and summed in bfloat16 or wider, within the bound.
A program may use at most 64 MiB of HBM per device.

```python
import math
import jax
import jax.numpy as jnp
import numpy as np
from jax import lax

L_DEV = 128
HD = 128
STEPS = 64
ROLLOUTS = 8
HEADS = 32
KV = 4
GROUP = 8
SEQ = 4096
HALF = 64
SPANS = 64
MOST_STEP = 512
N_CTX = 32


def draw_queries(key, part):
    key = jax.random.fold_in(key, 31)
    result = jnp.clip(2.0 * jax.random.normal(key, (SEQ, HEADS, HD), jnp.float32), -6.0, 6.0)
    return result.astype(jnp.bfloat16)


def draw_key_rows(key, part):
    key = jax.random.fold_in(key, 37)
    result = jnp.clip(jax.random.normal(key, (SEQ, KV, HD), jnp.float32), -6.0, 6.0)
    return result.astype(jnp.bfloat16)


def draw_token_pos(key, part):
    key = jax.random.fold_in(key, 43)
    chosen = jax.random.permutation(key, N_CTX)
    flipped = jax.random.randint(jax.random.fold_in(key, 1), (N_CTX,), 0, 2)
    row_index = jnp.arange(SEQ, dtype=jnp.int32)
    shard = row_index // L_DEV
    local = row_index % L_DEV
    first = local < HALF
    lower = chosen[shard]
    upper = SPANS - 1 - lower
    take_lower = first == (flipped[shard] == 0)
    span = jnp.where(take_lower, lower, upper)
    return (span * HALF + local % HALF).astype(jnp.int32)


def touch_ends(values, stream_key, least, top_value):
    dims = values.shape
    index_at = [jax.random.randint(jax.random.fold_in(stream_key, axis), (), 0, dims[axis]) for axis in range(len(dims))]
    values = values.at[tuple(index_at)].set(least)
    longest = dims.index(max(dims))
    index_at[longest] = (index_at[longest] + 1) % dims[longest]
    return values.at[tuple(index_at)].set(top_value)


def levels(stream_key, extent, cuts, least, largest):
    loudness = 1.0
    for dim, parts in cuts:
        heights = jax.random.uniform(jax.random.fold_in(jax.random.fold_in(stream_key, 6), dim), (parts,), jnp.float32, least / len(cuts), largest / len(cuts))
        loudness = loudness * jnp.repeat(jnp.exp(heights), extent[dim] // parts).reshape((-1,) + (1,) * (len(extent) - 1 - dim))
    return loudness


def length_profile(amount, total, reach, slope):
    weights = [(1 << 20) // math.isqrt(rank ** slope) + 1 for rank in range(2, amount + 1)]
    surplus, holding = total - reach - (amount - 1), [1] * (amount - 1)
    while surplus > 0:
        candidates = [i for i in range(amount - 1) if holding[i] < reach]
        whole, remaining = sum([weights[i] for i in candidates]), surplus
        for i in candidates:
            addition = min(reach - holding[i], max(1, remaining * weights[i] // whole), surplus)
            holding[i] = holding[i] + addition
            surplus = surplus - addition
    return np.array([reach] + holding)


def uneven(key, number_of, total, reach, skew):
    if number_of == 2:
        one = jax.random.randint(key, (), max(1, total - reach), min(reach, total - 1) + 1)
        return jnp.stack([one, total - one])
    lengths = jnp.asarray(length_profile(number_of, total, reach, skew), jnp.int32)
    twos = (number_of - 1) // 2
    source_of, taker = lengths[1:1 + 2 * twos:2], lengths[2:2 + 2 * twos:2]
    slack = jnp.minimum(source_of - 1, reach - taker)
    passed = jax.random.randint(jax.random.fold_in(key, 1), (twos,), 0, 1 << 20) % (slack + 1)
    lengths = lengths.at[1:1 + 2 * twos:2].set(source_of - passed).at[2:2 + 2 * twos:2].set(taker + passed)
    return lengths[jax.random.permutation(jax.random.fold_in(key, 2), number_of)]


def normal_values(stream_key, shape, scale, bound, shards=(), kind=jnp.bfloat16):
    values = jax.random.normal(stream_key, shape, jnp.float32) * scale
    if len(shards) > 0:
        values = levels(stream_key, shape, shards, -0.22, 0.18) * values
    return jnp.clip(values, min=-bound, max=bound).astype(kind)


def setup_inputs(seed: int = 0, part: int = 0) -> dict:
    seeds = jax.random.split(jax.random.key(seed), 9)
    own_keys = jax.random.split(jax.random.fold_in(seeds[8], part), 9)
    return {
        "queries": draw_queries(jax.random.fold_in(jax.random.fold_in(seeds[8], part), 71), part),
        "key_rows": draw_key_rows(jax.random.fold_in(jax.random.fold_in(seeds[8], part), 71), part),
        "value_rows": normal_values(own_keys[2], (SEQ, KV, HD), 1.0, 6.0, ((0, 32), (1, 4))),
        "token_pos": draw_token_pos(jax.random.fold_in(jax.random.fold_in(seeds[8], part), 71), part),
        "step_len": uneven(own_keys[4], STEPS, SEQ, MOST_STEP, 2).astype(jnp.int32),
        "label_count": touch_ends(jax.random.randint(own_keys[5], (STEPS,), 0, ROLLOUTS + 1), jax.random.fold_in(own_keys[5], 1), 0, ROLLOUTS).astype(jnp.int32),
        "out_grad": normal_values(own_keys[6], (SEQ, HEADS, HD), 2.0, 8.0, ((0, 32), (1, 4))),
        "reward_weight": normal_values(seeds[7], (HEADS, HD), 0.2, 1.25, ((0, 4),)),
    }


NEG_FILL = -1e+30

def reference(queries, key_rows, value_rows, token_pos, step_len, label_count, out_grad, reward_weight):
    score_scale = 1.0 / math.sqrt(HD)
    visible = token_pos[None, :] <= token_pos[:, None]

    def forward_head(head_index):
        query_head = queries[:, head_index]
        key_head = key_rows[:, head_index // GROUP]
        value_head = value_rows[:, head_index // GROUP]
        raw = jnp.dot(query_head, key_head.T, preferred_element_type=jnp.float32) * score_scale
        masked = jnp.where(visible, raw, NEG_FILL)
        top = lax.optimization_barrier(jnp.max(masked, axis=-1))
        weights = jnp.where(visible, jnp.exp(masked - top[:, None]), 0.0)
        row_total = lax.optimization_barrier(jnp.sum(weights, axis=-1))
        summed = jnp.dot(weights.astype(jnp.bfloat16), value_head, preferred_element_type=jnp.float32)
        attended = (summed / row_total[:, None]).astype(jnp.bfloat16)
        return (attended, top + jnp.log(row_total))
    attended, log_total = lax.map(forward_head, jnp.arange(HEADS, dtype=jnp.int32))
    position_row = jnp.zeros((SEQ,), jnp.int32).at[token_pos].set(jnp.arange(SEQ, dtype=jnp.int32))
    boundary = (jnp.cumsum(step_len) - 1).astype(jnp.int32)
    boundary_row = position_row[boundary]
    picked = attended[:, boundary_row].astype(jnp.float32)
    weight_wide = reward_weight.astype(jnp.float32)
    logits = jnp.einsum('hsd,hd->s', picked, weight_wide, precision=lax.Precision.HIGHEST)
    target = label_count.astype(jnp.float32) / ROLLOUTS
    step_loss = jax.nn.softplus(logits) - target * logits
    misfit = jax.nn.sigmoid(logits) - target
    d_reward = jnp.einsum('s,hsd->hd', misfit, picked, precision=lax.Precision.HIGHEST)
    row_weight = jnp.zeros((SEQ,), jnp.float32).at[boundary_row].add(misfit)
    grad_heads = (out_grad.astype(jnp.float32).transpose(1, 0, 2) + row_weight[None, :, None] * weight_wide[:, None, :]).astype(jnp.bfloat16)
    delta_rows = lax.optimization_barrier(jnp.sum(grad_heads.astype(jnp.float32) * attended.astype(jnp.float32), axis=-1))

    def backward_head(head_index):
        query_head = queries[:, head_index]
        key_head = key_rows[:, head_index // GROUP]
        value_head = value_rows[:, head_index // GROUP]
        grad_head = grad_heads[head_index]
        raw = jnp.dot(query_head, key_head.T, preferred_element_type=jnp.float32) * score_scale
        back_prob = jnp.exp(jnp.where(visible, raw - log_total[head_index][:, None], NEG_FILL))
        grad_prob = jnp.dot(grad_head, value_head.T, preferred_element_type=jnp.float32)
        grad_score = (back_prob * (grad_prob - delta_rows[head_index][:, None]) * score_scale).astype(jnp.bfloat16)
        query_part = jnp.dot(grad_score, key_head, preferred_element_type=jnp.float32).astype(jnp.bfloat16)
        key_part = jnp.dot(grad_score.T, query_head, preferred_element_type=jnp.float32)
        value_part = jnp.dot(back_prob.astype(jnp.bfloat16).T, grad_head, preferred_element_type=jnp.float32)
        return (query_part, key_part, value_part)
    query_grad, key_part, value_part = lax.map(backward_head, jnp.arange(HEADS, dtype=jnp.int32))
    d_query = query_grad.transpose(1, 0, 2)
    d_key = key_part.reshape(KV, GROUP, SEQ, HD).sum(axis=1).transpose(1, 0, 2).astype(jnp.bfloat16)
    d_value = value_part.reshape(KV, GROUP, SEQ, HD).sum(axis=1).transpose(1, 0, 2).astype(jnp.bfloat16)
    return (step_loss, d_query, d_key, d_value, d_reward)
```

```python
import functools
import math

import jax
import jax.numpy as jnp
from jax import lax
from jax.experimental import pallas as pl
from jax.experimental.pallas import tpu as pltpu
from jax.sharding import PartitionSpec as P

MESH = pl.DeviceIdType.MESH
F32, BF16 = jnp.float32, jnp.bfloat16
NX = 4
HD = 128
LD = 128
GROUP = 8
HALF = 64
ROWS = LD * GROUP
RHALF = HALF * GROUP
META = 16
STEPS = 64
ROLLOUTS = 8
SCALE = 1.0 / math.sqrt(HD)
LOG2E = math.log2(math.e)
C2 = SCALE * LOG2E
NEG = -1e30
A, B = slice(0, RHALF), slice(RHALF, ROWS)
EXACT = lax.Precision.HIGHEST


def nn(a, b, precision=None):
    return lax.dot_general(a, b, (((1,), (0,)), ((), ())), precision=precision, preferred_element_type=F32)


def nt(a, b, precision=None):
    return lax.dot_general(a, b, (((1,), (1,)), ((), ())), precision=precision, preferred_element_type=F32)


def tn(a, b):
    return lax.dot_general(a, b, (((0,), (0,)), ((), ())), preferred_element_type=F32)


def col_max(s):
    return jnp.max(s, axis=0, keepdims=True)


def col_sum(s):
    return jnp.sum(s, axis=0, keepdims=True)


def kernel(
    nz, nh,
    pos_ref, step_ref, label_ref, rw_ref, q_ref, g_ref, k_ref, v_ref,
    loss_ref, dq_ref, dk_ref, dv_ref, dr_ref,
    k_all, v_all, qn, qt, gn, gt, rwt, top_s, tot_s, out_s, dq_s, lse_s, delta_s,
    hx, tx, tz, tmine,
    s_kr, r_kr, s_kl, r_kl, p_k, s_kx, r_kx,
    p_v, f_v, c_v, r_v1, r_v2, s_vr, r_vr, s_vl, r_vl, dk_d, dv_d,
    send_sem, k_sem, v_sem, h_sem, tx_sem, tz_sem,
    kr_sem, kl_sem, kx_sem, fv_sem, v1_sem, v2_sem, vr_sem, vl_sem,
):
    far = nz // 2
    me = lax.axis_index("ctx")
    hd = lax.axis_index("head")
    z, x = me // NX, me % NX

    def zi(dz):
        return lax.rem(z + (dz + nz), nz)

    def xi(dx):
        return lax.rem(x + (dx + NX), NX)

    def xdev(dx):
        return {"ctx": z * NX + xi(dx)}

    def zdev(dz):
        return {"ctx": zi(dz) * NX + x}

    def hdev(dh):
        return {"head": lax.rem(hd + dh, nh)}

    def slot(dz, dx):
        return zi(dz) * NX + xi(dx)

    sends = []

    def send(src, dst, recv, dev):
        copy = pltpu.make_async_remote_copy(
            src_ref=src, dst_ref=dst, send_sem=send_sem.at[len(sends)], recv_sem=recv,
            device_id=dev, device_id_type=MESH,
        )
        copy.start()
        sends.append(copy)

    def arrived(dst, recv):
        pltpu.make_async_remote_copy(
            src_ref=dst, dst_ref=dst, send_sem=send_sem.at[0], recv_sem=recv,
            device_id=xdev(1), device_id_type=MESH,
        ).wait_recv()

    def send_k(at, dev):
        send(k_all.at[at], k_all.at[at], k_sem.at[at], dev)

    def send_v(at, dev):
        send(v_all.at[at], v_all.at[at], v_sem.at[at], dev)

    pos = pos_ref[...].astype(F32)
    first, second = pos[:, 0:1], pos[:, HALF:HALF + 1]
    span_f = jnp.minimum(first, second) * (1.0 / HALF)
    later_first = jnp.where(first > second, 1.0, 0.0)

    def ordered(value):
        n = value.shape[0] // 2
        one, two = value[:n].astype(F32), value[n:].astype(F32)
        swap = jnp.broadcast_to(later_first, one.shape) > 0.5
        return jnp.where(swap, two, one).astype(BF16), jnp.where(swap, one, two).astype(BF16)

    k_all[me, 0:HALF], k_all[me, HALF:LD] = ordered(k_ref[...])
    k_all[me, LD:] = jnp.broadcast_to(span_f, (META, HD)).astype(BF16)
    v_all[me, 0:HALF], v_all[me, HALF:LD] = ordered(v_ref[...])

    barrier = pltpu.get_barrier_semaphore()
    peers = [xdev(d) for d in range(1, NX)] + [zdev(d) for d in range(1, nz)] + [hdev(d) for d in range(1, nh)]
    for dev in peers:
        pl.semaphore_signal(barrier, inc=1, device_id=dev, device_id_type=MESH)
    pl.semaphore_wait(barrier, len(peers))

    for dx in (1, 3, 2):
        send_k(me, xdev(dx))
    send_k(me, zdev(1))
    send_k(me, zdev(-1))
    send_v(me, zdev(1))
    send_v(me, zdev(-1))
    send_v(me, xdev(1))
    send_v(me, xdev(-1))

    qn[A], qn[B] = ordered(q_ref[...])
    gn[A], gn[B] = ordered(g_ref[...])
    qt[...] = qn[...].T
    gt[...] = gn[...].T
    rw = rw_ref[...].astype(F32)
    rwt[...] = jnp.broadcast_to(rw[None], (LD, GROUP, HD)).reshape(ROWS, HD).T
    key_tok = lax.broadcasted_iota(jnp.int32, (HALF, RHALF), 0)
    row_tok = lax.broadcasted_iota(jnp.int32, (HALF, RHALF), 1) // GROUP
    tri = jnp.where(key_tok <= row_tok, 0.0, NEG)
    for rows, keys in ((A, slice(0, HALF)), (B, slice(HALF, LD))):
        s = nn(k_all[me, keys], qt[:, rows]) + tri
        top = col_max(s)
        p = jnp.exp2((s - top) * C2)
        top_s[:, rows] = top
        tot_s[:, rows] = col_sum(p)
        out_s[:, rows] = tn(v_all[me, keys], p.astype(BF16))

    def keys_of(ref, zz, half):
        return ref[pl.ds(zz * NX, NX), half * HALF:(half + 1) * HALF, :].reshape(NX * HALF, HD)

    def bias_of(zz, earlier):
        runs = k_all[pl.ds(zz * NX, NX), LD:, :].astype(F32)[:, 0:8, :]
        seen = (runs < span_f) if earlier else (runs > span_f)
        bias = jnp.where(seen, 0.0, NEG)
        bias = jnp.concatenate([bias] * (RHALF // HD), axis=-1)
        return jnp.broadcast_to(bias[:, None], (NX, HALF // 8, 8, RHALF)).reshape(NX * HALF, RHALF)

    def attend(dz):
        zz = zi(dz)
        kl, ku, vl, vu = (keys_of(r, zz, h) for r in (k_all, v_all) for h in (0, 1))
        s = nn(kl, qt[:, A]) + bias_of(zz, True)
        old = top_s[:, A]
        top = jnp.maximum(old, col_max(s))
        p = jnp.exp2((s - top) * C2)
        keep = jnp.exp2((old - top) * C2)
        top_s[:, A] = top
        tot_s[:, A] = tot_s[:, A] * keep + col_sum(p)
        out_s[:, A] = out_s[:, A] * keep + tn(vl, p.astype(BF16))
        s1 = nn(kl, qt[:, B])
        s2 = nn(ku, qt[:, B]) + bias_of(zz, False)
        old = top_s[:, B]
        top = jnp.maximum(old, jnp.maximum(col_max(s1), col_max(s2)))
        p1 = jnp.exp2((s1 - top) * C2)
        p2 = jnp.exp2((s2 - top) * C2)
        keep = jnp.exp2((old - top) * C2)
        top_s[:, B] = top
        tot_s[:, B] = tot_s[:, B] * keep + (col_sum(p1) + col_sum(p2))
        out_s[:, B] = out_s[:, B] * keep + (tn(vl, p1.astype(BF16)) + tn(vu, p2.astype(BF16)))

    def ring(s):
        return [0] if s == 0 else ([far] if s == far else [-s, s])

    def take_k(s):
        if s == 0:
            for dx in (1, 3, 2):
                at = slot(0, dx)
                arrived(k_all.at[at], k_sem.at[at])
                send_k(at, zdev(1))
                send_k(at, zdev(-1))
            return
        for xx in range(NX):
            for dz in ring(s):
                at = zi(dz) * NX + xx
                arrived(k_all.at[at], k_sem.at[at])
                if s + 1 < far or (s + 1 == far and (xx < NX // 2) == (dz < 0)):
                    send_k(at, zdev(1 if dz < 0 else -1))

    def take_vz(s):
        for dz in ring(s):
            at = slot(dz, 0)
            arrived(v_all.at[at], v_sem.at[at])
            if s + 1 < far or (s + 1 == far and dz < 0):
                send_v(at, zdev(1 if dz < 0 else -1))
            send_v(at, xdev(1))
            send_v(at, xdev(-1))

    def take_vx(s):
        for dz in ring(s):
            for dx in (-1, 1):
                at = slot(dz, dx)
                arrived(v_all.at[at], v_sem.at[at])
                if (dz % 2 == 0) == (dx < 0):
                    send_v(at, xdev(-dx))

    def take_v2(dz):
        at = slot(dz, 2)
        arrived(v_all.at[at], v_sem.at[at])

    for s in range(far + 1):
        take_k(s)
        if s + 1 <= far:
            take_vz(s + 1)
        take_vx(s)
        if s:
            for dz in ring(s - 1):
                take_v2(dz)
                attend(dz)
    take_v2(far)
    attend(far)

    total = tot_s[...]
    att = (out_s[...] * (1.0 / total)).astype(BF16).astype(F32)
    out_s[...] = att
    lse_s[...] = top_s[...] * C2 + jnp.log2(total)
    row_of = lax.broadcasted_iota(jnp.int32, (ROWS, LD), 0)
    tok_of = lax.broadcasted_iota(jnp.int32, (ROWS, LD), 1)
    gather_tok = jnp.where(row_of // GROUP == tok_of, 1.0, 0.0)
    score = nn(jnp.broadcast_to(col_sum(att * rwt[...]), (8, ROWS)), gather_tok, EXACT)
    hx[hd] = score
    for dh in range(1, nh):
        send(hx.at[hd], hx.at[hd], h_sem.at[hd], hdev(dh))
    s_of = lax.broadcasted_iota(jnp.int32, (STEPS, STEPS), 0)
    t_of = lax.broadcasted_iota(jnp.int32, (STEPS, STEPS), 1)
    lens = jnp.broadcast_to(step_ref[...].astype(F32), (STEPS, STEPS))
    ends = jnp.sum(jnp.where(t_of <= s_of, lens, 0.0), axis=1, keepdims=True) - 1.0
    lane = lax.broadcasted_iota(jnp.int32, (1, LD), 1)
    last_span = nz * NX * 2 - 1
    run = jnp.where(lane < HALF, span_f, last_span - span_f)
    tok_pos = run * HALF + (lane % HALF).astype(F32)
    owned = jnp.where(ends == tok_pos, 1.0, 0.0)
    target = label_ref[...].astype(F32) / ROLLOUTS
    tok_target = nn(jnp.broadcast_to(target, (8, STEPS)), owned, EXACT)
    is_end = col_sum(owned)
    for dh in range(1, nh):
        at = lax.rem(hd + dh, nh)
        arrived(hx.at[at], h_sem.at[at])
    logit = hx[0]
    for h in range(1, nh):
        logit = logit + hx[h]
    misfit = (jax.nn.sigmoid(logit) - tok_target) * is_end
    row_of = lax.broadcasted_iota(jnp.int32, (LD, ROWS), 1)
    tok_of = lax.broadcasted_iota(jnp.int32, (LD, ROWS), 0)
    spread = jnp.where(row_of // GROUP == tok_of, 1.0, 0.0)
    weight = nn(misfit, spread, EXACT)[0:1]
    grad = (gt[...].astype(F32) + weight * rwt[...]).astype(BF16)
    gt[...] = grad
    gn[...] = grad.T
    delta_s[...] = col_sum(grad.astype(F32) * att)
    head_of = lax.broadcasted_iota(jnp.int32, (GROUP, ROWS), 0)
    row_of = lax.broadcasted_iota(jnp.int32, (GROUP, ROWS), 1)
    pick = jnp.where(row_of % GROUP == head_of, 1.0, 0.0)
    tmine[0:8] = nt(pick, att * weight, EXACT)
    own_logits = nt(logit, owned, EXACT)
    tmine[8:16] = jnp.concatenate([own_logits, jnp.zeros_like(own_logits)], axis=1)
    tx[x] = tmine[...]
    for dx in (1, 3, 2):
        send(tx.at[x], tx.at[x], tx_sem.at[x], xdev(dx))

    def totals_x():
        for dx in (1, 3, 2):
            at = xi(dx)
            arrived(tx.at[at], tx_sem.at[at])
        tz[z] = tx[0] + tx[1] + tx[2] + tx[3]
        for dz in range(1, nz):
            send(tz.at[z], tz.at[z], tz_sem.at[z], zdev(dz))

    def totals_z():
        for dz in range(1, nz):
            at = zi(dz)
            arrived(tz.at[at], tz_sem.at[at])
        both = tz[0]
        for i in range(1, nz):
            both = both + tz[i]
        dr_ref[...] = both[0:8]
        logits = both[8:9, 0:STEPS]
        soft = jnp.maximum(logits, 0.0) + jnp.log1p(jnp.exp(-jnp.abs(logits)))
        loss_ref[...] = soft - target * logits

    dq_s[...] = jnp.zeros(dq_s.shape, F32)

    def back(k, v, rows, bias):
        s = nn(k, qt[:, rows])
        if bias is not None:
            s = s + bias
        p = jnp.exp2(s * C2 - lse_s[:, rows])
        ds = (p * (nn(v, gt[:, rows]) - delta_s[:, rows])).astype(BF16)
        dq_s[:, rows] += tn(k, ds)
        return nn(ds, qn[rows]), nn(p.astype(BF16), gn[rows])

    def back_group(dz):
        zz = zi(dz)
        kl, ku, vl, vu = (keys_of(r, zz, h) for r in (k_all, v_all) for h in (0, 1))
        k1, v1 = back(kl, vl, A, bias_of(zz, True))
        k2, v2 = back(kl, vl, B, None)
        k3, v3 = back(ku, vu, B, bias_of(zz, False))
        p_k[:, 0:HALF] = ((k1 + k2) * SCALE).reshape(NX, HALF, HD)
        p_k[:, HALF:LD] = (k3 * SCALE).reshape(NX, HALF, HD)
        return (v1 + v2).reshape(NX, HALF, HD), v3.reshape(NX, HALF, HD)

    def wide(ref):
        return ref[...].astype(F32)

    order = [far]
    for s in range(far - 1, 0, -1):
        order += [s, -s]
    order += [0]
    two = NX // 2

    def pass_k(dz):
        if dz == far:
            s_kr[far, 0:two] = p_k[0:two].astype(BF16)
            s_kl[far, two:] = p_k[two:].astype(BF16)
            send(s_kr.at[far, 0:two], r_kr.at[far, 0:two], kr_sem.at[far, 0], zdev(1))
            send(s_kl.at[far, two:], r_kl.at[far, two:], kl_sem.at[far, 1], zdev(-1))
            return
        d = abs(dz)
        s_k, r_k, sem = (s_kr, r_kr, kr_sem) if dz > 0 else (s_kl, r_kl, kl_sem)
        for half in (0, 1):
            part = slice(half * two, (half + 1) * two)
            own = p_k[part]
            if d + 1 < far or (half == 0) == (dz > 0):
                arrived(r_k.at[d + 1, part], sem.at[d + 1, half])
                own = own + wide(r_k.at[d + 1, part])
            s_k[d, part] = own.astype(BF16)
            send(s_k.at[d, part], r_k.at[d, part], sem.at[d, half], zdev(1 if dz > 0 else -1))

    def give_v(i):
        way = 1 if order[i] % 2 == 0 else -1
        send(p_v.at[i, xi(2)], f_v.at[i], fv_sem.at[i], xdev(way))
        send(p_v.at[i, xi(-way)], r_v1.at[i], v1_sem.at[i], xdev(-way))

    def relay_v(i):
        way = 1 if order[i] % 2 == 0 else -1
        arrived(f_v.at[i], fv_sem.at[i])
        c_v[i] = (p_v[i, xi(way)].astype(F32) + wide(f_v.at[i])).astype(BF16)
        send(c_v.at[i], r_v2.at[i], v2_sem.at[i], xdev(way))

    def pass_v(i):
        dz = order[i]
        arrived(r_v1.at[i], v1_sem.at[i])
        arrived(r_v2.at[i], v2_sem.at[i])
        total = p_v[i, x].astype(F32) + wide(r_v1.at[i]) + wide(r_v2.at[i])
        if dz > 0:
            if dz < far:
                arrived(r_vr.at[dz + 1], vr_sem.at[dz + 1])
                total = total + wide(r_vr.at[dz + 1])
            s_vr[dz] = total.astype(BF16)
            send(s_vr.at[dz], r_vr.at[dz], vr_sem.at[dz], zdev(1))
        elif dz < 0:
            d = -dz
            if d + 1 < far:
                arrived(r_vl.at[d + 1], vl_sem.at[d + 1])
                total = total + wide(r_vl.at[d + 1])
            s_vl[d] = total.astype(BF16)
            send(s_vl.at[d], r_vl.at[d], vl_sem.at[d], zdev(-1))
        else:
            arrived(r_vr.at[1], vr_sem.at[1])
            arrived(r_vl.at[1], vl_sem.at[1])
            dv_d[...] += total + wide(r_vr.at[1]) + wide(r_vl.at[1])

    for i, dz in enumerate(order):
        v_lo, v_hi = back_group(dz)
        p_v[i, :, 0:HALF] = v_lo.astype(BF16)
        p_v[i, :, HALF:LD] = v_hi.astype(BF16)
        give_v(i)
        if dz:
            pass_k(dz)
        if i >= 1:
            relay_v(i - 1)
        if i >= 2:
            pass_v(i - 2)
        if i == 1:
            totals_x()
    last = len(order) - 1
    relay_v(last)
    for half in (0, 1):
        part = slice(half * two, (half + 1) * two)
        arrived(r_kr.at[1, part], kr_sem.at[1, half])
        arrived(r_kl.at[1, part], kl_sem.at[1, half])
    s_kx[...] = (p_k[...] + wide(r_kr.at[1]) + wide(r_kl.at[1])).astype(BF16)
    for dx in (1, 3, 2):
        send(s_kx.at[xi(dx)], r_kx.at[dx], kx_sem.at[dx], xdev(dx))
    pass_v(last - 1)
    for rows, keys in ((A, slice(0, HALF)), (B, slice(HALF, LD))):
        dk_own, dv_own = back(k_all[me, keys], v_all[me, keys], rows, tri)
        dk_d[keys], dv_d[keys] = dk_own * SCALE, dv_own
    dq_ref[A], dq_ref[B] = ordered((dq_s[...] * SCALE).T)
    pass_v(last)
    dv_ref[0:HALF], dv_ref[HALF:LD] = ordered(dv_d[...])
    totals_z()
    for dx in (1, 3, 2):
        arrived(r_kx.at[dx], kx_sem.at[dx])
    dk_d[...] += s_kx[x].astype(F32) + wide(r_kx.at[1]) + wide(r_kx.at[2]) + wide(r_kx.at[3])
    dk_ref[0:HALF], dk_ref[HALF:LD] = ordered(dk_d[...])
    for copy in sends:
        copy.wait_send()


def local(nz, nh, queries, key_rows, value_rows, token_pos, step_len, label_count, out_grad, reward_weight):
    far, n = nz // 2, nz * NX
    vmem = pl.BlockSpec(memory_space=pltpu.VMEM)
    block = (LD, HD)
    scratch = [
        ((n, LD + META, HD), BF16), ((n,) + block, BF16),
        ((ROWS, HD), BF16), ((HD, ROWS), BF16), ((ROWS, HD), BF16), ((HD, ROWS), BF16), ((HD, ROWS), F32),
        ((1, ROWS), F32), ((1, ROWS), F32), ((HD, ROWS), F32), ((HD, ROWS), F32), ((1, ROWS), F32), ((1, ROWS), F32),
        ((nh, 8, HD), F32), ((NX, 16, HD), F32), ((nz, 16, HD), F32), ((16, HD), F32),
    ]
    chain = ((far + 1, NX) + block, BF16)
    scratch += [chain] * 4 + [((NX,) + block, F32), ((NX,) + block, BF16), ((NX,) + block, BF16)]
    steps = ((nz,) + block, BF16)
    scratch += [((nz, NX) + block, BF16), steps, steps, steps, steps] + [((far + 1,) + block, BF16)] * 4
    scratch += [(block, F32), (block, F32)]
    dma = lambda *shape: pltpu.SemaphoreType.DMA(shape)
    sems = [
        dma(256), dma(n), dma(n), dma(nh), dma(NX), dma(nz),
        dma(far + 1, 2), dma(far + 1, 2), dma(NX), dma(nz), dma(nz), dma(nz), dma(far + 1), dma(far + 1),
    ]
    loss, dq, dk, dv, dr = pl.pallas_call(
        functools.partial(kernel, nz, nh),
        out_shape=[
            jax.ShapeDtypeStruct((1, STEPS), F32),
            jax.ShapeDtypeStruct((ROWS, HD), BF16),
            jax.ShapeDtypeStruct(block, BF16),
            jax.ShapeDtypeStruct(block, BF16),
            jax.ShapeDtypeStruct((GROUP, HD), F32),
        ],
        in_specs=[vmem] * 8,
        out_specs=[vmem] * 5,
        scratch_shapes=[pltpu.VMEM(s, t) for s, t in scratch] + sems,
        compiler_params=pltpu.CompilerParams(
            collective_id=0, has_side_effects=True, vmem_limit_bytes=48 * 2**20
        ),
    )(
        token_pos.reshape(1, LD),
        step_len.reshape(1, STEPS),
        label_count.reshape(1, STEPS),
        reward_weight,
        queries.reshape(ROWS, HD),
        out_grad.reshape(ROWS, HD),
        key_rows.reshape(block),
        value_rows.reshape(block),
    )
    return (
        loss.reshape(STEPS),
        dq.reshape(queries.shape),
        dk.reshape(key_rows.shape),
        dv.reshape(value_rows.shape),
        dr,
    )


def solution(mesh):
    rows = P(("dp", "ctx"), "head", None)
    return jax.shard_map(
        functools.partial(local, mesh.shape["ctx"] // NX, mesh.shape["head"]),
        mesh=mesh,
        in_specs=(rows, rows, rows, P(("dp", "ctx")), P("dp"), P("dp"), rows, P("head", None)),
        out_specs=(P("dp"), rows, rows, rows, P(("dp", "head"), None)),
        check_vma=False,
    )
```

```python
import functools
import math

import jax
import jax.numpy as jnp
from jax import lax
from jax.experimental import pallas as pl
from jax.experimental.pallas import tpu as pltpu
from jax.sharding import PartitionSpec as P

MESH = pl.DeviceIdType.MESH
F32, BF16 = jnp.float32, jnp.bfloat16
NX = 4
HD = 128
LD = 128
GROUP = 8
HALF = 64
ROWS = LD * GROUP
RHALF = HALF * GROUP
META = 16
STEPS = 64
ROLLOUTS = 8
SCALE = 1.0 / math.sqrt(HD)
LOG2E = math.log2(math.e)
C2 = SCALE * LOG2E
NEG = -1e30
A, B = slice(0, RHALF), slice(RHALF, ROWS)
VMEM_BYTES = 60 * 2**20
OTHERS = (1, 3, 2)


def nn(a, b):
    return lax.dot_general(a, b, (((1,), (0,)), ((), ())), preferred_element_type=F32)


def nt(a, b):
    return lax.dot_general(a, b, (((1,), (1,)), ((), ())), preferred_element_type=F32)


def tn(a, b):
    return lax.dot_general(a, b, (((0,), (0,)), ((), ())), preferred_element_type=F32)


def col_max(s):
    return jnp.max(s, axis=0, keepdims=True)


def col_sum(s):
    return jnp.sum(s, axis=0, keepdims=True)


def kernel(
    nz, nh,
    pos_hbm, step_hbm, label_hbm, rw_hbm, q_hbm, g_hbm, k_hbm, v_hbm,
    loss_hbm, dq_hbm, dk_hbm, dv_hbm, dr_hbm,
    loss_ref, dq_ref, dk_ref, dv_ref, dr_ref, pos_ref, step_ref, label_ref, rw_ref, q_ref, g_ref, k_ref, v_ref,
    k_all, v_all, qn, qt, gn, gt, rwt, top_s, tot_s, out_s, dq_s, lse_s, delta_s,
    to_tok, to_row, owned_s, hx, tx, tz,
    s_kr, r_kr, s_kl, r_kl, p_k, s_kx, r_kx,
    p_v, r_v, s_vr, r_vr, s_vl, r_vl, dk_d, dv_d,
    in_sem, out_sem, send_sem, k_sem, v_sem, h_sem, tx_sem, tz_sem,
    kr_sem, kl_sem, kx_sem, rv_sem, vr_sem, vl_sem,
):
    far = nz // 2
    me = lax.axis_index("ctx")
    hd = lax.axis_index("head")
    z, x = me // NX, me % NX

    def zi(dz):
        return lax.rem(z + (dz + nz), nz)

    def xi(dx):
        return lax.rem(x + (dx + NX), NX)

    def xdev(dx):
        return {"ctx": z * NX + xi(dx)}

    def zdev(dz):
        return {"ctx": zi(dz) * NX + x}

    def hdev(dh):
        return {"head": lax.rem(hd + dh, nh)}

    def slot(dz, dx):
        return zi(dz) * NX + xi(dx)

    sends, stores = [], []

    def store(src, dst):
        copy = pltpu.make_async_copy(src, dst, out_sem.at[len(stores)])
        copy.start()
        stores.append(copy)

    def send(src, dst, recv, dev):
        copy = pltpu.make_async_remote_copy(
            src_ref=src, dst_ref=dst, send_sem=send_sem.at[len(sends)], recv_sem=recv,
            device_id=dev, device_id_type=MESH,
        )
        copy.start()
        sends.append(copy)

    def arrived(dst, recv):
        pltpu.make_async_remote_copy(
            src_ref=dst, dst_ref=dst, send_sem=send_sem.at[0], recv_sem=recv,
            device_id=xdev(1), device_id_type=MESH,
        ).wait_recv()

    def send_k(at, dev):
        send(k_all.at[at], k_all.at[at], k_sem.at[at], dev)

    def send_v(at, dev):
        send(v_all.at[at], v_all.at[at], v_sem.at[at], dev)

    barrier = pltpu.get_barrier_semaphore()
    peers = [xdev(d) for d in range(1, NX)] + [zdev(d) for d in range(1, nz)] + [hdev(d) for d in range(1, nh)]
    for dev in peers:
        pl.semaphore_signal(barrier, inc=1, device_id=dev, device_id_type=MESH)
    pairs = [
        (pos_hbm, pos_ref), (k_hbm, k_ref), (v_hbm, v_ref), (q_hbm, q_ref), (g_hbm, g_ref),
        (rw_hbm, rw_ref), (step_hbm, step_ref), (label_hbm, label_ref),
    ]
    loads = [pltpu.make_async_copy(src, dst, in_sem.at[i]) for i, (src, dst) in enumerate(pairs)]
    for load in loads:
        load.start()

    for load in loads[0:3]:
        load.wait()
    pos = pos_ref[...].astype(F32)
    first, second = pos[:, 0:1], pos[:, HALF:HALF + 1]
    span_f = jnp.minimum(first, second) * (1.0 / HALF)
    later_first = jnp.where(first > second, 1.0, 0.0)

    def ordered(value):
        n = value.shape[0] // 2
        one, two = value[:n].astype(F32), value[n:].astype(F32)
        swap = jnp.broadcast_to(later_first, one.shape) > 0.5
        return jnp.where(swap, two, one).astype(BF16), jnp.where(swap, one, two).astype(BF16)

    k_all[me, 0:HALF], k_all[me, HALF:LD] = ordered(k_ref[...])
    k_all[me, LD:] = jnp.broadcast_to(span_f, (META, HD)).astype(BF16)
    v_all[me, 0:HALF], v_all[me, HALF:LD] = ordered(v_ref[...])

    pl.semaphore_wait(barrier, len(peers))

    for give in (send_k, send_v):
        give(me, zdev(1))
        give(me, zdev(-1))
        for dx in OTHERS:
            give(me, xdev(dx))

    for load in loads[3:]:
        load.wait()
    qn[A], qn[B] = ordered(q_ref[...])
    gn[A], gn[B] = ordered(g_ref[...])
    qt[...] = qn[...].T
    gt[...] = gn[...].T
    key_tok = lax.broadcasted_iota(jnp.int32, (HALF, RHALF), 0)
    row_tok = lax.broadcasted_iota(jnp.int32, (HALF, RHALF), 1) // GROUP
    tri = jnp.where(key_tok <= row_tok, 0.0, NEG)
    for rows, keys in ((A, slice(0, HALF)), (B, slice(HALF, LD))):
        s = nn(k_all[me, keys], qt[:, rows]) + tri
        top = col_max(s)
        p = jnp.exp2((s - top) * C2)
        top_s[:, rows] = top
        tot_s[:, rows] = col_sum(p)
        out_s[:, rows] = tn(v_all[me, keys], p.astype(BF16))

    def keys_of(ref, zz, half):
        return ref[pl.ds(zz * NX, NX), half * HALF:(half + 1) * HALF, :].reshape(NX * HALF, HD)

    def bias_of(zz, earlier):
        runs = k_all[pl.ds(zz * NX, NX), LD:, :].astype(F32)[:, 0:8, :]
        seen = (runs < span_f) if earlier else (runs > span_f)
        bias = jnp.where(seen, 0.0, NEG)
        bias = jnp.concatenate([bias] * (RHALF // HD), axis=-1)
        return jnp.broadcast_to(bias[:, None], (NX, HALF // 8, 8, RHALF)).reshape(NX * HALF, RHALF)

    def attend_a(dz):
        zz = zi(dz)
        kl, vl = keys_of(k_all, zz, 0), keys_of(v_all, zz, 0)
        s = nn(kl, qt[:, A]) + bias_of(zz, True)
        old = top_s[:, A]
        top = jnp.maximum(old, col_max(s))
        p = jnp.exp2((s - top) * C2)
        keep = jnp.exp2((old - top) * C2)
        top_s[:, A] = top
        tot_s[:, A] = tot_s[:, A] * keep + col_sum(p)
        out_s[:, A] = out_s[:, A] * keep + tn(vl, p.astype(BF16))

    def attend_b(dz):
        zz = zi(dz)
        kl, ku, vl, vu = (keys_of(r, zz, h) for r in (k_all, v_all) for h in (0, 1))
        s1 = nn(kl, qt[:, B])
        s2 = nn(ku, qt[:, B]) + bias_of(zz, False)
        old = top_s[:, B]
        top = jnp.maximum(old, jnp.maximum(col_max(s1), col_max(s2)))
        p1 = jnp.exp2((s1 - top) * C2)
        p2 = jnp.exp2((s2 - top) * C2)
        keep = jnp.exp2((old - top) * C2)
        top_s[:, B] = top
        tot_s[:, B] = tot_s[:, B] * keep + (col_sum(p1) + col_sum(p2))
        out_s[:, B] = out_s[:, B] * keep + (tn(vl, p1.astype(BF16)) + tn(vu, p2.astype(BF16)))

    def ring(s):
        return [0] if s == 0 else ([far] if s == far else [-s, s])

    def take_k(dz, dx):
        at = slot(dz, dx)
        arrived(k_all.at[at], k_sem.at[at])
        s = abs(dz)
        if s == 0:
            send_k(at, zdev(1))
            send_k(at, zdev(-1))
        elif s + 1 < far or (s + 1 == far and (dx < NX // 2) == (dz < 0)):
            send_k(at, zdev(1 if dz < 0 else -1))

    def take_vz(s):
        for dz in ring(s):
            at = slot(dz, 0)
            arrived(v_all.at[at], v_sem.at[at])
            if s + 1 < far or (s + 1 == far and dz < 0):
                send_v(at, zdev(1 if dz < 0 else -1))
        for dz in ring(s):
            for dx in OTHERS:
                send_v(slot(dz, 0), xdev(dx))

    def take_vx(dz):
        for dx in OTHERS:
            at = slot(dz, dx)
            arrived(v_all.at[at], v_sem.at[at])

    def prepare():
        rw = rw_ref[...].astype(F32)
        rwt[...] = jnp.broadcast_to(rw[None], (LD, GROUP, HD)).reshape(ROWS, HD).T
        row_of = lax.broadcasted_iota(jnp.int32, (ROWS, LD), 0)
        tok_of = lax.broadcasted_iota(jnp.int32, (ROWS, LD), 1)
        to_tok[...] = jnp.where(row_of // GROUP == tok_of, 1.0, 0.0).astype(BF16)
        row_of = lax.broadcasted_iota(jnp.int32, (LD, ROWS), 1)
        tok_of = lax.broadcasted_iota(jnp.int32, (LD, ROWS), 0)
        to_row[...] = jnp.where(row_of // GROUP == tok_of, 1.0, 0.0).astype(BF16)
        s_of = lax.broadcasted_iota(jnp.int32, (STEPS, STEPS), 0)
        t_of = lax.broadcasted_iota(jnp.int32, (STEPS, STEPS), 1)
        lens = jnp.broadcast_to(step_ref[...].astype(F32), (STEPS, STEPS))
        ends = jnp.sum(jnp.where(t_of <= s_of, lens, 0.0), axis=1, keepdims=True) - 1.0
        lane = lax.broadcasted_iota(jnp.int32, (1, LD), 1)
        run = jnp.where(lane < HALF, span_f, (nz * NX * 2 - 1) - span_f)
        tok_pos = run * HALF + (lane % HALF).astype(F32)
        owned_s[...] = jnp.where(ends == tok_pos, 1.0, 0.0)
        dq_s[...] = jnp.zeros(dq_s.shape, F32)

    for s in range(far + 1):
        pieces = []
        if s == 1:
            take_vx(0)
        if s:
            for dz in ring(s - 1):
                pieces += [(attend_a, dz), (attend_b, dz)]
        for i, dx in enumerate((0,) + OTHERS):
            for dz in ring(s):
                if s or dx:
                    take_k(dz, dx)
            if i == 0 and s + 1 <= far:
                take_vz(s + 1)
            if i < len(pieces):
                piece, dz = pieces[i]
                if piece is attend_a and dz:
                    take_vx(dz)
                piece(dz)
        if s == far:
            prepare()
    take_vx(far)
    attend_a(far)
    attend_b(far)

    total = tot_s[...]
    att = (out_s[...] * (1.0 / total)).astype(BF16).astype(F32)
    out_s[...] = att
    lse_s[...] = top_s[...] * C2 + jnp.log2(total)
    def thirds(value):
        one = value.astype(BF16)
        rest = value - one.astype(F32)
        two = rest.astype(BF16)
        return [one, two, (rest - two.astype(F32)).astype(BF16)]

    def rows_of(value):
        pad = jnp.zeros((META - 3,) + value.shape[1:], F32)
        return jnp.concatenate([t.astype(F32) for t in thirds(value)] + [pad], axis=0).astype(BF16)

    score = col_sum(nn(rows_of(col_sum(att * rwt[...])), to_tok[...]))
    hx[hd] = jnp.broadcast_to(score, (8, LD))
    for dh in range(1, nh):
        send(hx.at[hd], hx.at[hd], h_sem.at[hd], hdev(dh))
    owned = owned_s[...]
    owned_low = owned.astype(BF16)
    target = label_ref[...].astype(F32) / ROLLOUTS
    tok_target = nn(jnp.broadcast_to(target, (META, STEPS)).astype(BF16), owned_low)[0:1]
    is_end = col_sum(owned)
    for dh in range(1, nh):
        at = lax.rem(hd + dh, nh)
        arrived(hx.at[at], h_sem.at[at])
    logit = hx[0]
    for h in range(1, nh):
        logit = logit + hx[h]
    logit = logit[0:1]
    misfit = (jax.nn.sigmoid(logit) - tok_target) * is_end
    weight = col_sum(nn(rows_of(misfit), to_row[...]))
    grad = (gt[...].astype(F32) + weight * rwt[...]).astype(BF16)
    gt[...] = grad
    gn[...] = grad.T
    delta_s[...] = col_sum(grad.astype(F32) * att)

    def totals():
        head_of = lax.broadcasted_iota(jnp.int32, (GROUP, ROWS), 0)
        row_of = lax.broadcasted_iota(jnp.int32, (GROUP, ROWS), 1)
        pick = jnp.where(row_of % GROUP == head_of, jnp.broadcast_to(weight, (GROUP, ROWS)), 0.0)
        att_low = out_s[...].astype(BF16)
        parts = [nt(t, att_low) for t in thirds(pick)]
        tx[x, 0:8] = parts[0] + parts[1] + parts[2]
        own = col_sum(nt(rows_of(logit), owned_low))
        tx[x, 8:16] = jnp.broadcast_to(jnp.concatenate([own, jnp.zeros_like(own)], axis=1), (8, LD))
        for dx in OTHERS:
            send(tx.at[x], tx.at[x], tx_sem.at[x], xdev(dx))

    def totals_x():
        for dx in OTHERS:
            at = xi(dx)
            arrived(tx.at[at], tx_sem.at[at])
        tz[z] = tx[0] + tx[1] + tx[2] + tx[3]
        for dz in range(1, nz):
            send(tz.at[z], tz.at[z], tz_sem.at[z], zdev(dz))

    def totals_z():
        for dz in range(1, nz):
            at = zi(dz)
            arrived(tz.at[at], tz_sem.at[at])
        both = tz[0]
        for i in range(1, nz):
            both = both + tz[i]
        dr_ref[...] = both[0:8]
        logits = both[8:9, 0:STEPS]
        soft = jnp.maximum(logits, 0.0) + jnp.log1p(jnp.exp(-jnp.abs(logits)))
        loss_ref[...] = soft - target * logits
        store(dr_ref, dr_hbm)
        store(loss_ref, loss_hbm)

    def back(k, v, rows, bias):
        s = nn(k, qt[:, rows])
        if bias is not None:
            s = s + bias
        p = jnp.exp2(s * C2 - lse_s[:, rows])
        ds = (p * (nn(v, gt[:, rows]) - delta_s[:, rows])).astype(BF16)
        dq_s[:, rows] += tn(k, ds)
        return nn(ds, qn[rows]), nn(p.astype(BF16), gn[rows])

    def back_group(dz):
        zz = zi(dz)
        kl, ku, vl, vu = (keys_of(r, zz, h) for r in (k_all, v_all) for h in (0, 1))
        k1, v1 = back(kl, vl, A, bias_of(zz, True))
        k2, v2 = back(kl, vl, B, None)
        k3, v3 = back(ku, vu, B, bias_of(zz, False))
        p_k[:, 0:HALF] = ((k1 + k2) * SCALE).reshape(NX, HALF, HD)
        p_k[:, HALF:LD] = (k3 * SCALE).reshape(NX, HALF, HD)
        return (v1 + v2).reshape(NX, HALF, HD), v3.reshape(NX, HALF, HD)

    def wide(ref):
        return ref[...].astype(F32)

    order = [far]
    for s in range(far - 1, 0, -1):
        order += [s, -s]
    order += [0]
    two = NX // 2

    def pass_k(dz):
        d = abs(dz)
        for xx in range(NX):
            for right in (True, False):
                crosses = (xx < two) == right
                if (dz == far and not crosses) or (dz != far and (dz > 0) != right):
                    continue
                s_k, r_k, sem = (s_kr, r_kr, kr_sem) if right else (s_kl, r_kl, kl_sem)
                own = p_k[xx]
                if d + 1 < far or (d + 1 == far and crosses):
                    arrived(r_k.at[d + 1, xx], sem.at[d + 1, xx])
                    own = own + wide(r_k.at[d + 1, xx])
                s_k[d, xx] = own.astype(BF16)
                send(s_k.at[d, xx], r_k.at[d, xx], sem.at[d, xx], zdev(1 if right else -1))

    def give_v(i):
        for dx in OTHERS:
            send(p_v.at[i, xi(dx)], r_v.at[i, dx], rv_sem.at[i, dx], xdev(dx))

    def pass_v(i):
        dz = order[i]
        total = p_v[i, x].astype(F32)
        for dx in OTHERS:
            arrived(r_v.at[i, dx], rv_sem.at[i, dx])
            total = total + wide(r_v.at[i, dx])
        if dz > 0:
            if dz < far:
                arrived(r_vr.at[dz + 1], vr_sem.at[dz + 1])
                total = total + wide(r_vr.at[dz + 1])
            s_vr[dz] = total.astype(BF16)
            send(s_vr.at[dz], r_vr.at[dz], vr_sem.at[dz], zdev(1))
        elif dz < 0:
            d = -dz
            if d + 1 < far:
                arrived(r_vl.at[d + 1], vl_sem.at[d + 1])
                total = total + wide(r_vl.at[d + 1])
            s_vl[d] = total.astype(BF16)
            send(s_vl.at[d], r_vl.at[d], vl_sem.at[d], zdev(-1))
        else:
            arrived(r_vr.at[1], vr_sem.at[1])
            arrived(r_vl.at[1], vl_sem.at[1])
            dv_d[...] += total + wide(r_vr.at[1]) + wide(r_vl.at[1])

    for i, dz in enumerate(order):
        v_lo, v_hi = back_group(dz)
        p_v[i, :, 0:HALF] = v_lo.astype(BF16)
        p_v[i, :, HALF:LD] = v_hi.astype(BF16)
        give_v(i)
        if dz:
            pass_k(dz)
        if i >= 2:
            pass_v(i - 2)
        if i == 0:
            totals()
        if i == 3:
            totals_x()
    last = len(order) - 1
    for rows, keys in ((A, slice(0, HALF)), (B, slice(HALF, LD))):
        dk_own, dv_own = back(k_all[me, keys], v_all[me, keys], rows, tri)
        dk_d[keys], dv_d[keys] = dk_own * SCALE, dv_own
    pass_v(last - 1)
    for dx in OTHERS + (0,):
        xx = xi(dx)
        arrived(r_kr.at[1, xx], kr_sem.at[1, xx])
        arrived(r_kl.at[1, xx], kl_sem.at[1, xx])
        total = p_k[xx] + r_kr[1, xx].astype(F32) + r_kl[1, xx].astype(F32)
        if dx:
            s_kx[xx] = total.astype(BF16)
            send(s_kx.at[xx], r_kx.at[dx], kx_sem.at[dx], xdev(dx))
        else:
            dk_d[...] += total
    dq_ref[A], dq_ref[B] = ordered((dq_s[...] * SCALE).T)
    store(dq_ref, dq_hbm)
    pass_v(last)
    dv_ref[0:HALF], dv_ref[HALF:LD] = ordered(dv_d[...])
    store(dv_ref, dv_hbm)
    totals_z()
    for dx in OTHERS:
        arrived(r_kx.at[dx], kx_sem.at[dx])
    dk_d[...] += wide(r_kx.at[1]) + wide(r_kx.at[2]) + wide(r_kx.at[3])
    dk_ref[0:HALF], dk_ref[HALF:LD] = ordered(dk_d[...])
    store(dk_ref, dk_hbm)
    for copy in sends:
        copy.wait_send()
    for copy in stores:
        copy.wait()


def hand_over(*refs):
    ins, outs, held, (in_sem, out_sem) = refs[:5], refs[5:10], refs[10:15], refs[15:]
    first = [pltpu.make_async_copy(ins[i], held[i], in_sem.at[i]) for i in range(5)]
    second = [pltpu.make_async_copy(held[i], outs[i], out_sem.at[i]) for i in range(5)]
    for copy in first:
        copy.start()
    for one, two in zip(first, second):
        one.wait()
        two.start()
    for copy in second:
        copy.wait()


def local(nz, nh, queries, key_rows, value_rows, token_pos, step_len, label_count, out_grad, reward_weight):
    far, n = nz // 2, nz * NX
    hbm = pl.BlockSpec(memory_space=pltpu.HBM)
    block = (LD, HD)
    results = [((1, STEPS), F32), ((ROWS, HD), BF16), (block, BF16), (block, BF16), ((GROUP, HD), F32)]
    shapes = [jax.ShapeDtypeStruct(s, t) for s, t in results]
    scratch = results + [
        ((1, LD), jnp.int32), ((1, STEPS), jnp.int32), ((1, STEPS), jnp.int32), ((GROUP, HD), BF16),
        ((ROWS, HD), BF16), ((ROWS, HD), BF16), (block, BF16), (block, BF16),
        ((n, LD + META, HD), BF16), ((n,) + block, BF16),
        ((ROWS, HD), BF16), ((HD, ROWS), BF16), ((ROWS, HD), BF16), ((HD, ROWS), BF16), ((HD, ROWS), F32),
        ((1, ROWS), F32), ((1, ROWS), F32), ((HD, ROWS), F32), ((HD, ROWS), F32), ((1, ROWS), F32), ((1, ROWS), F32),
        ((ROWS, LD), BF16), ((LD, ROWS), BF16), ((STEPS, LD), F32),
        ((nh, 8, HD), F32), ((NX, 16, HD), F32), ((nz, 16, HD), F32),
    ]
    chain = ((far + 1, NX) + block, BF16)
    scratch += [chain] * 4 + [((NX,) + block, F32), ((NX,) + block, BF16), ((NX,) + block, BF16)]
    scratch += [((nz, NX) + block, BF16), ((nz, NX) + block, BF16)] + [((far + 1,) + block, BF16)] * 4
    scratch += [(block, F32), (block, F32)]
    dma = lambda *shape: pltpu.SemaphoreType.DMA(shape)
    sems = [
        dma(8), dma(5), dma(256), dma(n), dma(n), dma(nh), dma(NX), dma(nz),
        dma(far + 1, NX), dma(far + 1, NX), dma(NX), dma(nz, NX), dma(far + 1), dma(far + 1),
    ]
    partial = pl.pallas_call(
        functools.partial(kernel, nz, nh),
        out_shape=shapes,
        in_specs=[hbm] * 8,
        out_specs=[hbm] * 5,
        scratch_shapes=[pltpu.VMEM(s, t) for s, t in scratch] + sems,
        compiler_params=pltpu.CompilerParams(
            collective_id=0, has_side_effects=True, vmem_limit_bytes=VMEM_BYTES
        ),
    )(
        token_pos.reshape(1, LD),
        step_len.reshape(1, STEPS),
        label_count.reshape(1, STEPS),
        reward_weight,
        queries.reshape(ROWS, HD),
        out_grad.reshape(ROWS, HD),
        key_rows.reshape(block),
        value_rows.reshape(block),
    )
    loss, dq, dk, dv, dr = pl.pallas_call(
        hand_over,
        out_shape=shapes,
        in_specs=[hbm] * 5,
        out_specs=[hbm] * 5,
        scratch_shapes=[pltpu.VMEM(s, t) for s, t in results] + [dma(5), dma(5)],
        compiler_params=pltpu.CompilerParams(vmem_limit_bytes=VMEM_BYTES),
    )(*partial)
    return (
        loss.reshape(STEPS),
        dq.reshape(queries.shape),
        dk.reshape(key_rows.shape),
        dv.reshape(value_rows.shape),
        dr,
    )


def solution(mesh):
    rows = P(("dp", "ctx"), "head", None)
    return jax.shard_map(
        functools.partial(local, mesh.shape["ctx"] // NX, mesh.shape["head"]),
        mesh=mesh,
        in_specs=(rows, rows, rows, P(("dp", "ctx")), P("dp"), P("dp"), rows, P("head", None)),
        out_specs=(P("dp"), rows, rows, rows, P(("dp", "head"), None)),
        check_vma=False,
    )
```

```python
import functools
import math

import jax
import jax.numpy as jnp
from jax import lax
from jax.experimental import pallas as pl
from jax.experimental.pallas import tpu as pltpu
from jax.sharding import PartitionSpec as P

MESH = pl.DeviceIdType.MESH
F32, BF16 = jnp.float32, jnp.bfloat16
NX = 4
HD = 128
LD = 128
GROUP = 8
HALF = 64
ROWS = LD * GROUP
RHALF = HALF * GROUP
META = 16
STEPS = 64
ROLLOUTS = 8
SCALE = 1.0 / math.sqrt(HD)
LOG2E = math.log2(math.e)
C2 = SCALE * LOG2E
NEG = -1e30
A, B = slice(0, RHALF), slice(RHALF, ROWS)
VMEM_BYTES = 60 * 2**20
OTHERS = (1, 3, 2)


def nn(a, b):
    return lax.dot_general(a, b, (((1,), (0,)), ((), ())), preferred_element_type=F32)


def nt(a, b):
    return lax.dot_general(a, b, (((1,), (1,)), ((), ())), preferred_element_type=F32)


def tn(a, b):
    return lax.dot_general(a, b, (((0,), (0,)), ((), ())), preferred_element_type=F32)


def col_max(s):
    return jnp.max(s, axis=0, keepdims=True)


def col_sum(s):
    return jnp.sum(s, axis=0, keepdims=True)


def kernel(
    nz, nh,
    pos_hbm, step_hbm, label_hbm, rw_hbm, q_hbm, g_hbm, k_hbm, v_hbm,
    loss_hbm, dq_hbm, dk_hbm, dv_hbm, dr_hbm,
    loss_ref, dq_ref, dk_ref, dv_ref, dr_ref, pos_ref, step_ref, label_ref, rw_ref, q_ref, g_ref, k_ref, v_ref,
    k_all, v_all, qn, qt, gn, gt, rwt, top_s, tot_s, out_s, dq_s, lse_s, delta_s,
    to_tok, to_row, owned_s, hx, tx, tz,
    held, p_k, s_k, r_k, s_kx, r_kx, p_v, r_v, s_v, r_v2, dk_d, dv_d,
    in_sem, out_sem, send_sem, k_sem, v_sem, h_sem, tx_sem, tz_sem,
    rk_sem, kx_sem, rv_sem, vz_sem,
):
    far = nz // 2
    me = lax.axis_index("ctx")
    hd = lax.axis_index("head")
    z, x = me // NX, me % NX

    def zi(dz):
        return lax.rem(z + (dz + nz), nz)

    def xi(dx):
        return lax.rem(x + (dx + NX), NX)

    def xdev(dx):
        return {"ctx": z * NX + xi(dx)}

    def zdev(dz):
        return {"ctx": zi(dz) * NX + x}

    def hdev(dh):
        return {"head": lax.rem(hd + dh, nh)}

    def slot(dz, dx):
        return zi(dz) * NX + xi(dx)

    sends, stores = [], []

    def store(src, dst):
        copy = pltpu.make_async_copy(src, dst, out_sem.at[len(stores)])
        copy.start()
        stores.append(copy)

    def send(src, dst, recv, dev):
        copy = pltpu.make_async_remote_copy(
            src_ref=src, dst_ref=dst, send_sem=send_sem.at[len(sends)], recv_sem=recv,
            device_id=dev, device_id_type=MESH,
        )
        copy.start()
        sends.append(copy)

    def arrived(dst, recv):
        pltpu.make_async_remote_copy(
            src_ref=dst, dst_ref=dst, send_sem=send_sem.at[0], recv_sem=recv,
            device_id=xdev(1), device_id_type=MESH,
        ).wait_recv()

    def send_k(at, dev):
        send(k_all.at[at], k_all.at[at], k_sem.at[at], dev)

    def send_v(at, dev):
        send(v_all.at[at], v_all.at[at], v_sem.at[at], dev)

    barrier = pltpu.get_barrier_semaphore()
    peers = [xdev(d) for d in range(1, NX)] + [zdev(d) for d in range(1, nz)] + [hdev(d) for d in range(1, nh)]
    for dev in peers:
        pl.semaphore_signal(barrier, inc=1, device_id=dev, device_id_type=MESH)
    pairs = [
        (pos_hbm, pos_ref), (k_hbm, k_ref), (v_hbm, v_ref), (q_hbm, q_ref), (g_hbm, g_ref),
        (rw_hbm, rw_ref), (step_hbm, step_ref), (label_hbm, label_ref),
    ]
    loads = [pltpu.make_async_copy(src, dst, in_sem.at[i]) for i, (src, dst) in enumerate(pairs)]
    for load in loads:
        load.start()

    for load in loads[0:3]:
        load.wait()
    pos = pos_ref[...].astype(F32)
    first, second = pos[:, 0:1], pos[:, HALF:HALF + 1]
    span_f = jnp.minimum(first, second) * (1.0 / HALF)
    later_first = jnp.where(first > second, 1.0, 0.0)

    def ordered(value):
        n = value.shape[0] // 2
        one, two = value[:n].astype(F32), value[n:].astype(F32)
        swap = jnp.broadcast_to(later_first, one.shape) > 0.5
        return jnp.where(swap, two, one).astype(BF16), jnp.where(swap, one, two).astype(BF16)

    k_all[me, 0:HALF], k_all[me, HALF:LD] = ordered(k_ref[...])
    k_all[me, LD:] = jnp.broadcast_to(span_f, (META, HD)).astype(BF16)
    v_all[me, 0:HALF], v_all[me, HALF:LD] = ordered(v_ref[...])

    pl.semaphore_wait(barrier, len(peers))

    for give in (send_k, send_v):
        give(me, zdev(1))
        give(me, zdev(-1))
        for dx in OTHERS:
            give(me, xdev(dx))

    for load in loads[3:]:
        load.wait()
    qn[A], qn[B] = ordered(q_ref[...])
    gn[A], gn[B] = ordered(g_ref[...])
    qt[...] = qn[...].T
    gt[...] = gn[...].T
    key_tok = lax.broadcasted_iota(jnp.int32, (HALF, RHALF), 0)
    row_tok = lax.broadcasted_iota(jnp.int32, (HALF, RHALF), 1) // GROUP
    tri = jnp.where(key_tok <= row_tok, 0.0, NEG)
    for rows, keys in ((A, slice(0, HALF)), (B, slice(HALF, LD))):
        s = nn(k_all[me, keys], qt[:, rows]) + tri
        top = col_max(s)
        p = jnp.exp2((s - top) * C2)
        top_s[:, rows] = top
        tot_s[:, rows] = col_sum(p)
        out_s[:, rows] = tn(v_all[me, keys], p.astype(BF16))

    def keys_of(ref, zz, half):
        return ref[pl.ds(zz * NX, NX), half * HALF:(half + 1) * HALF, :].reshape(NX * HALF, HD)

    def bias_of(zz, earlier):
        runs = k_all[pl.ds(zz * NX, NX), LD:, :].astype(F32)[:, 0:8, :]
        seen = (runs < span_f) if earlier else (runs > span_f)
        bias = jnp.where(seen, 0.0, NEG)
        bias = jnp.concatenate([bias] * (RHALF // HD), axis=-1)
        return jnp.broadcast_to(bias[:, None], (NX, HALF // 8, 8, RHALF)).reshape(NX * HALF, RHALF)

    def attend_a(dz):
        zz = zi(dz)
        kl, vl = keys_of(k_all, zz, 0), keys_of(v_all, zz, 0)
        s = nn(kl, qt[:, A]) + bias_of(zz, True)
        old = top_s[:, A]
        top = jnp.maximum(old, col_max(s))
        p = jnp.exp2((s - top) * C2)
        keep = jnp.exp2((old - top) * C2)
        top_s[:, A] = top
        tot_s[:, A] = tot_s[:, A] * keep + col_sum(p)
        out_s[:, A] = out_s[:, A] * keep + tn(vl, p.astype(BF16))

    def attend_b(dz):
        zz = zi(dz)
        kl, ku, vl, vu = (keys_of(r, zz, h) for r in (k_all, v_all) for h in (0, 1))
        s1 = nn(kl, qt[:, B])
        s2 = nn(ku, qt[:, B]) + bias_of(zz, False)
        old = top_s[:, B]
        top = jnp.maximum(old, jnp.maximum(col_max(s1), col_max(s2)))
        p1 = jnp.exp2((s1 - top) * C2)
        p2 = jnp.exp2((s2 - top) * C2)
        keep = jnp.exp2((old - top) * C2)
        top_s[:, B] = top
        tot_s[:, B] = tot_s[:, B] * keep + (col_sum(p1) + col_sum(p2))
        out_s[:, B] = out_s[:, B] * keep + (tn(vl, p1.astype(BF16)) + tn(vu, p2.astype(BF16)))

    def ring(s):
        return [0] if s == 0 else ([far] if s == far else [-s, s])

    def take_k(dz, dx):
        at = slot(dz, dx)
        arrived(k_all.at[at], k_sem.at[at])
        s = abs(dz)
        if s == 0:
            send_k(at, zdev(1))
            send_k(at, zdev(-1))
        elif s + 1 < far or (s + 1 == far and (dx < NX // 2) == (dz < 0)):
            send_k(at, zdev(1 if dz < 0 else -1))

    def take_vz(s):
        for dz in ring(s):
            at = slot(dz, 0)
            arrived(v_all.at[at], v_sem.at[at])
            if s + 1 < far or (s + 1 == far and dz < 0):
                send_v(at, zdev(1 if dz < 0 else -1))
        for dz in ring(s):
            for dx in OTHERS:
                send_v(slot(dz, 0), xdev(dx))

    def take_vx(dz):
        for dx in OTHERS:
            at = slot(dz, dx)
            arrived(v_all.at[at], v_sem.at[at])

    def prepare():
        rw = rw_ref[...].astype(F32)
        rwt[...] = jnp.broadcast_to(rw[None], (LD, GROUP, HD)).reshape(ROWS, HD).T
        row_of = lax.broadcasted_iota(jnp.int32, (ROWS, LD), 0)
        tok_of = lax.broadcasted_iota(jnp.int32, (ROWS, LD), 1)
        to_tok[...] = jnp.where(row_of // GROUP == tok_of, 1.0, 0.0).astype(BF16)
        row_of = lax.broadcasted_iota(jnp.int32, (LD, ROWS), 1)
        tok_of = lax.broadcasted_iota(jnp.int32, (LD, ROWS), 0)
        to_row[...] = jnp.where(row_of // GROUP == tok_of, 1.0, 0.0).astype(BF16)
        s_of = lax.broadcasted_iota(jnp.int32, (STEPS, STEPS), 0)
        t_of = lax.broadcasted_iota(jnp.int32, (STEPS, STEPS), 1)
        lens = jnp.broadcast_to(step_ref[...].astype(F32), (STEPS, STEPS))
        ends = jnp.sum(jnp.where(t_of <= s_of, lens, 0.0), axis=1, keepdims=True) - 1.0
        lane = lax.broadcasted_iota(jnp.int32, (1, LD), 1)
        run = jnp.where(lane < HALF, span_f, (nz * NX * 2 - 1) - span_f)
        tok_pos = run * HALF + (lane % HALF).astype(F32)
        owned_s[...] = jnp.where(ends == tok_pos, 1.0, 0.0)
        dq_s[...] = jnp.zeros(dq_s.shape, F32)

    for s in range(far + 1):
        pieces = []
        if s == 1:
            take_vx(0)
        if s:
            for dz in ring(s - 1):
                pieces += [(attend_a, dz), (attend_b, dz)]
        for i, dx in enumerate((0,) + OTHERS):
            for dz in ring(s):
                if s or dx:
                    take_k(dz, dx)
            if i == 0 and s + 1 <= far:
                take_vz(s + 1)
            if i < len(pieces):
                piece, dz = pieces[i]
                if piece is attend_a and dz:
                    take_vx(dz)
                piece(dz)
        if s == far:
            prepare()
    take_vx(far)
    attend_a(far)
    attend_b(far)

    total = tot_s[...]
    att = (out_s[...] * (1.0 / total)).astype(BF16).astype(F32)
    out_s[...] = att
    lse_s[...] = top_s[...] * C2 + jnp.log2(total)
    def thirds(value):
        one = value.astype(BF16)
        rest = value - one.astype(F32)
        two = rest.astype(BF16)
        return [one, two, (rest - two.astype(F32)).astype(BF16)]

    def rows_of(value):
        pad = jnp.zeros((META - 3,) + value.shape[1:], F32)
        return jnp.concatenate([t.astype(F32) for t in thirds(value)] + [pad], axis=0).astype(BF16)

    score = col_sum(nn(rows_of(col_sum(att * rwt[...])), to_tok[...]))
    hx[hd] = jnp.broadcast_to(score, (8, LD))
    for dh in range(1, nh):
        send(hx.at[hd], hx.at[hd], h_sem.at[hd], hdev(dh))
    early = [far, far - 1, 1 - far]

    def blocks(dz):
        zz = zi(dz)
        kl, ku, vl, vu = (keys_of(r, zz, h) for r in (k_all, v_all) for h in (0, 1))
        return ((kl, vl, A, bias_of(zz, True)), (kl, vl, B, None), (ku, vu, B, bias_of(zz, False)))

    def prob_of(k, rows, bias):
        s = nn(k, qt[:, rows])
        if bias is not None:
            s = s + bias
        return jnp.exp2(s * C2 - lse_s[:, rows])

    for j, dz in enumerate(early):
        for b, (k, _, rows, bias) in enumerate(blocks(dz)):
            held[j, b] = prob_of(k, rows, bias)
    owned = owned_s[...]
    owned_low = owned.astype(BF16)
    target = label_ref[...].astype(F32) / ROLLOUTS
    tok_target = nn(jnp.broadcast_to(target, (META, STEPS)).astype(BF16), owned_low)[0:1]
    is_end = col_sum(owned)
    for dh in range(1, nh):
        at = lax.rem(hd + dh, nh)
        arrived(hx.at[at], h_sem.at[at])
    logit = hx[0]
    for h in range(1, nh):
        logit = logit + hx[h]
    logit = logit[0:1]
    misfit = (jax.nn.sigmoid(logit) - tok_target) * is_end
    weight = col_sum(nn(rows_of(misfit), to_row[...]))
    grad = (gt[...].astype(F32) + weight * rwt[...]).astype(BF16)
    gt[...] = grad
    gn[...] = grad.T
    delta_s[...] = col_sum(grad.astype(F32) * att)

    def totals():
        head_of = lax.broadcasted_iota(jnp.int32, (GROUP, ROWS), 0)
        row_of = lax.broadcasted_iota(jnp.int32, (GROUP, ROWS), 1)
        pick = jnp.where(row_of % GROUP == head_of, jnp.broadcast_to(weight, (GROUP, ROWS)), 0.0)
        att_low = out_s[...].astype(BF16)
        parts = [nt(t, att_low) for t in thirds(pick)]
        tx[x, 0:8] = parts[0] + parts[1] + parts[2]
        own = col_sum(nt(rows_of(logit), owned_low))
        tx[x, 8:16] = jnp.broadcast_to(jnp.concatenate([own, jnp.zeros_like(own)], axis=1), (8, LD))
        for dx in OTHERS:
            send(tx.at[x], tx.at[x], tx_sem.at[x], xdev(dx))

    def totals_x():
        for dx in OTHERS:
            at = xi(dx)
            arrived(tx.at[at], tx_sem.at[at])
        tz[z] = tx[0] + tx[1] + tx[2] + tx[3]
        for dz in range(1, nz):
            send(tz.at[z], tz.at[z], tz_sem.at[z], zdev(dz))

    def totals_z():
        for dz in range(1, nz):
            at = zi(dz)
            arrived(tz.at[at], tz_sem.at[at])
        both = tz[0]
        for i in range(1, nz):
            both = both + tz[i]
        dr_ref[...] = both[0:8]
        logits = both[8:9, 0:STEPS]
        soft = jnp.maximum(logits, 0.0) + jnp.log1p(jnp.exp(-jnp.abs(logits)))
        loss_ref[...] = soft - target * logits
        store(dr_ref, dr_hbm)
        store(loss_ref, loss_hbm)

    def back(k, v, rows, p):
        ds = (p * (nn(v, gt[:, rows]) - delta_s[:, rows])).astype(BF16)
        dq_s[:, rows] += tn(k, ds)
        return nn(ds, qn[rows]), nn(p.astype(BF16), gn[rows])

    def back_group(dz):
        (k1, v1), (k2, v2), (k3, v3) = (
            back(k, v, rows, held[early.index(dz), b] if dz in early else prob_of(k, rows, bias))
            for b, (k, v, rows, bias) in enumerate(blocks(dz))
        )
        whole = (NX, HALF, HD)
        return ((k1 + k2) * SCALE).reshape(whole), (k3 * SCALE).reshape(whole), (v1 + v2).reshape(whole), v3.reshape(whole)

    def wide(ref):
        return ref[...].astype(F32)

    FAR, THREE, MID, ONE, OWN = range(5)
    turns = (2,) + tuple(d for d in OTHERS if d != 2) + (0,)

    def comes(level, w, j):
        return level != FAR or (j < NX // 2) == (w == 0)

    def to_owner(level, ways, add=None):
        for j, dx in enumerate(turns):
            for w in ways:
                if not comes(level, w, j):
                    continue
                total = p_k[level, 0 if level == FAR else w, xi(dx)]
                for other in add or ():
                    if comes(other, w, j):
                        total = total + got_k(other, w, j)
                s_k[level, w, j] = total.astype(BF16)
                hops = 2 if level == FAR else 1
                send(s_k.at[level, w, j], r_k.at[level, w, j], rk_sem.at[level, w, j], zdev(-hops if w else hops))

    def got_k(level, w, j):
        arrived(r_k.at[level, w, j], rk_sem.at[level, w, j])
        return wide(r_k.at[level, w, j])

    def give_v(level):
        for dx in OTHERS:
            if level in (FAR, OWN):
                send(p_v.at[level, xi(dx), 0], r_v.at[level, dx, 0], rv_sem.at[level, dx], xdev(dx))
            else:
                send(p_v.at[level, xi(dx)], r_v.at[level, dx], rv_sem.at[level, dx], xdev(dx))

    def sum_v(level):
        one = level in (FAR, OWN)
        total = p_v[level, x, 0].astype(F32) if one else p_v[level, x].astype(F32)
        for dx in OTHERS:
            ref = r_v.at[level, dx, 0] if one else r_v.at[level, dx]
            arrived(ref, rv_sem.at[level, dx])
            total = total + wide(ref)
        return total

    def got_v(level, w):
        arrived(r_v2.at[level, w], vz_sem.at[level, w])
        return wide(r_v2.at[level, w])

    def pass_v(level):
        total = sum_v(level)
        if level == FAR:
            s_v[FAR, 0] = total.astype(BF16)
            send(s_v.at[FAR, 0], r_v2.at[FAR, 0], vz_sem.at[FAR, 0], zdev(2))
            return
        right, left = total[0], total[1]
        if level == MID:
            right = right + got_v(THREE, 0) + got_v(FAR, 0)
            left = left + got_v(THREE, 1)
        if level == ONE:
            right, left = right + got_v(MID, 0), left + got_v(MID, 1)
        for w, value in ((0, right), (1, left)):
            s_v[level, w] = value.astype(BF16)
            send(s_v.at[level, w], r_v2.at[level, w], vz_sem.at[level, w], zdev(-1 if w else 1))

    def group(level, right=True):
        dz = {FAR: far, THREE: 3, MID: 2, ONE: 1, OWN: 0}[level] * (1 if right else -1)
        w = 0 if right else 1
        k_lo, k_hi, v_lo, v_hi = back_group(dz)
        p_v[level, :, w, 0:HALF] = v_lo.astype(BF16)
        p_v[level, :, w, HALF:LD] = v_hi.astype(BF16)
        p_k[level, w, :, 0:HALF], p_k[level, w, :, HALF:LD] = k_lo, k_hi

    group(FAR)
    to_owner(FAR, (0, 1))
    give_v(FAR)
    group(THREE)
    to_owner(THREE, (0,))
    group(THREE, False)
    to_owner(THREE, (1,))
    give_v(THREE)
    group(MID)
    group(MID, False)
    give_v(MID)
    pass_v(FAR)
    to_owner(MID, (0, 1), (THREE, FAR))
    group(ONE)
    totals()
    pass_v(THREE)
    group(ONE, False)
    give_v(ONE)
    to_owner(ONE, (0, 1), (MID,))
    group(OWN)
    give_v(OWN)
    totals_x()
    pass_v(MID)
    for rows, keys in ((A, slice(0, HALF)), (B, slice(HALF, LD))):
        k_own = k_all[me, keys]
        dk_own, dv_own = back(k_own, v_all[me, keys], rows, prob_of(k_own, rows, tri))
        dk_d[keys], dv_d[keys] = dk_own * SCALE, dv_own
    pass_v(ONE)
    for j, dx in enumerate(turns):
        total = p_k[OWN, 0, xi(dx)] + got_k(ONE, 0, j) + got_k(ONE, 1, j)
        if dx:
            s_kx[dx] = total.astype(BF16)
            send(s_kx.at[dx], r_kx.at[dx], kx_sem.at[dx], xdev(dx))
        else:
            dk_d[...] += total
    dq_ref[A], dq_ref[B] = ordered((dq_s[...] * SCALE).T)
    store(dq_ref, dq_hbm)
    dv_d[...] += sum_v(OWN) + got_v(ONE, 0) + got_v(ONE, 1)
    dv_ref[0:HALF], dv_ref[HALF:LD] = ordered(dv_d[...])
    store(dv_ref, dv_hbm)
    totals_z()
    for dx in OTHERS:
        arrived(r_kx.at[dx], kx_sem.at[dx])
    dk_d[...] += wide(r_kx.at[1]) + wide(r_kx.at[2]) + wide(r_kx.at[3])
    dk_ref[0:HALF], dk_ref[HALF:LD] = ordered(dk_d[...])
    store(dk_ref, dk_hbm)
    for copy in sends:
        copy.wait_send()
    for copy in stores:
        copy.wait()


def hand_over(*refs):
    ins, outs, held, (in_sem, out_sem) = refs[:5], refs[5:10], refs[10:15], refs[15:]
    first = [pltpu.make_async_copy(ins[i], held[i], in_sem.at[i]) for i in range(5)]
    second = [pltpu.make_async_copy(held[i], outs[i], out_sem.at[i]) for i in range(5)]
    for copy in first:
        copy.start()
    for one, two in zip(first, second):
        one.wait()
        two.start()
    for copy in second:
        copy.wait()


def local(nz, nh, queries, key_rows, value_rows, token_pos, step_len, label_count, out_grad, reward_weight):
    n = nz * NX
    hbm = pl.BlockSpec(memory_space=pltpu.HBM)
    block = (LD, HD)
    results = [((1, STEPS), F32), ((ROWS, HD), BF16), (block, BF16), (block, BF16), ((GROUP, HD), F32)]
    shapes = [jax.ShapeDtypeStruct(s, t) for s, t in results]
    scratch = results + [
        ((1, LD), jnp.int32), ((1, STEPS), jnp.int32), ((1, STEPS), jnp.int32), ((GROUP, HD), BF16),
        ((ROWS, HD), BF16), ((ROWS, HD), BF16), (block, BF16), (block, BF16),
        ((n, LD + META, HD), BF16), ((n,) + block, BF16),
        ((ROWS, HD), BF16), ((HD, ROWS), BF16), ((ROWS, HD), BF16), ((HD, ROWS), BF16), ((HD, ROWS), F32),
        ((1, ROWS), F32), ((1, ROWS), F32), ((HD, ROWS), F32), ((HD, ROWS), F32), ((1, ROWS), F32), ((1, ROWS), F32),
        ((ROWS, LD), BF16), ((LD, ROWS), BF16), ((STEPS, LD), F32),
        ((nh, 8, HD), F32), ((NX, 16, HD), F32), ((nz, 16, HD), F32),
    ]
    four = (NX,) + block
    scratch += [
        ((3, 3, NX * HALF, RHALF), F32), ((5, 2) + four, F32),
        ((4, 2) + four, BF16), ((4, 2) + four, BF16), (four, BF16), (four, BF16),
        ((5, NX, 2) + block, BF16), ((5, NX, 2) + block, BF16), ((4, 2) + block, BF16), ((4, 2) + block, BF16),
    ]
    scratch += [(block, F32), (block, F32)]
    dma = lambda *shape: pltpu.SemaphoreType.DMA(shape)
    sems = [
        dma(8), dma(5), dma(256), dma(n), dma(n), dma(nh), dma(NX), dma(nz),
        dma(4, 2, NX), dma(NX), dma(5, NX), dma(4, 2),
    ]
    partial = pl.pallas_call(
        functools.partial(kernel, nz, nh),
        out_shape=shapes,
        in_specs=[hbm] * 8,
        out_specs=[hbm] * 5,
        scratch_shapes=[pltpu.VMEM(s, t) for s, t in scratch] + sems,
        compiler_params=pltpu.CompilerParams(
            collective_id=0, has_side_effects=True, vmem_limit_bytes=VMEM_BYTES
        ),
    )(
        token_pos.reshape(1, LD),
        step_len.reshape(1, STEPS),
        label_count.reshape(1, STEPS),
        reward_weight,
        queries.reshape(ROWS, HD),
        out_grad.reshape(ROWS, HD),
        key_rows.reshape(block),
        value_rows.reshape(block),
    )
    loss, dq, dk, dv, dr = pl.pallas_call(
        hand_over,
        out_shape=shapes,
        in_specs=[hbm] * 5,
        out_specs=[hbm] * 5,
        scratch_shapes=[pltpu.VMEM(s, t) for s, t in results] + [dma(5), dma(5)],
        compiler_params=pltpu.CompilerParams(vmem_limit_bytes=VMEM_BYTES),
    )(*partial)
    return (
        loss.reshape(STEPS),
        dq.reshape(queries.shape),
        dk.reshape(key_rows.shape),
        dv.reshape(value_rows.shape),
        dr,
    )


def solution(mesh):
    rows = P(("dp", "ctx"), "head", None)
    return jax.shard_map(
        functools.partial(local, mesh.shape["ctx"] // NX, mesh.shape["head"]),
        mesh=mesh,
        in_specs=(rows, rows, rows, P(("dp", "ctx")), P("dp"), P("dp"), rows, P("head", None)),
        out_specs=(P("dp"), rows, rows, rows, P(("dp", "head"), None)),
        check_vma=False,
    )
```

```python
import functools
import math

import jax
import jax.numpy as jnp
from jax import lax
from jax.experimental import pallas as pl
from jax.experimental.pallas import tpu as pltpu
from jax.sharding import PartitionSpec as P

MESH = pl.DeviceIdType.MESH
F32, BF16 = jnp.float32, jnp.bfloat16
NX = 4
HD = 128
LD = 128
GROUP = 8
HALF = 64
ROWS = LD * GROUP
RHALF = HALF * GROUP
META = 16
STEPS = 64
ROLLOUTS = 8
SCALE = 1.0 / math.sqrt(HD)
LOG2E = math.log2(math.e)
C2 = SCALE * LOG2E
NEG = -1e30
A, B = slice(0, RHALF), slice(RHALF, ROWS)
VMEM_BYTES = 60 * 2**20
OTHERS = (1, 3, 2)


def nn(a, b):
    return lax.dot_general(a, b, (((1,), (0,)), ((), ())), preferred_element_type=F32)


def nt(a, b):
    return lax.dot_general(a, b, (((1,), (1,)), ((), ())), preferred_element_type=F32)


def tn(a, b):
    return lax.dot_general(a, b, (((0,), (0,)), ((), ())), preferred_element_type=F32)


def col_max(s):
    return jnp.max(s, axis=0, keepdims=True)


def col_sum(s):
    return jnp.sum(s, axis=0, keepdims=True)


def kernel(
    nz, nh,
    pos_hbm, step_hbm, label_hbm, rw_hbm, q_hbm, g_hbm, k_hbm, v_hbm,
    loss_hbm, dq_hbm, dk_hbm, dv_hbm, dr_hbm,
    loss_ref, dq_ref, dk_ref, dv_ref, dr_ref, pos_ref, step_ref, label_ref, rw_ref, q_ref, g_ref, k_ref, v_ref,
    k_all, v_all, qn, qt, gn, gt, rwt, top_s, tot_s, out_s, dq_s, lse_s, delta_s,
    to_tok, to_row, owned_s, hx, tx, tz,
    held, p_k, s_k, r_k, s_kx, r_kx, p_v, r_v, s_v, r_v2, dk_d, dv_d,
    in_sem, out_sem, send_sem, k_sem, v_sem, h_sem, tx_sem, tz_sem,
    rk_sem, kx_sem, rv_sem, vz_sem,
):
    far = nz // 2
    me = lax.axis_index("ctx")
    hd = lax.axis_index("head")
    z, x = me // NX, me % NX

    def zi(dz):
        return lax.rem(z + (dz + nz), nz)

    def xi(dx):
        return lax.rem(x + (dx + NX), NX)

    def xdev(dx):
        return {"ctx": z * NX + xi(dx)}

    def zdev(dz):
        return {"ctx": zi(dz) * NX + x}

    def hdev(dh):
        return {"head": lax.rem(hd + dh, nh)}

    def slot(dz, dx):
        return zi(dz) * NX + xi(dx)

    sends, stores = [], []

    def store(src, dst):
        copy = pltpu.make_async_copy(src, dst, out_sem.at[len(stores)])
        copy.start()
        stores.append(copy)

    def send(src, dst, recv, dev):
        copy = pltpu.make_async_remote_copy(
            src_ref=src, dst_ref=dst, send_sem=send_sem.at[len(sends)], recv_sem=recv,
            device_id=dev, device_id_type=MESH,
        )
        copy.start()
        sends.append(copy)

    def arrived(dst, recv):
        pltpu.make_async_remote_copy(
            src_ref=dst, dst_ref=dst, send_sem=send_sem.at[0], recv_sem=recv,
            device_id=xdev(1), device_id_type=MESH,
        ).wait_recv()

    def send_k(at, dev):
        send(k_all.at[at], k_all.at[at], k_sem.at[at], dev)

    def send_v(at, dev):
        send(v_all.at[at], v_all.at[at], v_sem.at[at], dev)

    pairs = [
        (pos_hbm, pos_ref), (k_hbm, k_ref), (v_hbm, v_ref), (q_hbm, q_ref), (g_hbm, g_ref),
        (rw_hbm, rw_ref), (step_hbm, step_ref), (label_hbm, label_ref),
    ]
    loads = [pltpu.make_async_copy(src, dst, in_sem.at[i]) for i, (src, dst) in enumerate(pairs)]
    for load in loads[0:3]:
        load.start()

    barrier = pltpu.get_barrier_semaphore()
    peers = [xdev(d) for d in range(1, NX)] + [zdev(d) for d in range(1, nz)] + [hdev(d) for d in range(1, nh)]
    for dev in peers:
        pl.semaphore_signal(barrier, inc=1, device_id=dev, device_id_type=MESH)
    for load in loads[3:]:
        load.start()
    for load in loads[0:3]:
        load.wait()
    pos = pos_ref[...].astype(F32)
    first, second = pos[:, 0:1], pos[:, HALF:HALF + 1]
    span_f = jnp.minimum(first, second) * (1.0 / HALF)
    later_first = jnp.where(first > second, 1.0, 0.0)

    def ordered(value):
        n = value.shape[0] // 2
        one, two = value[:n].astype(F32), value[n:].astype(F32)
        swap = jnp.broadcast_to(later_first, one.shape) > 0.5
        return jnp.where(swap, two, one).astype(BF16), jnp.where(swap, one, two).astype(BF16)

    k_all[me, 0:HALF], k_all[me, HALF:LD] = ordered(k_ref[...])
    k_all[me, LD:] = jnp.broadcast_to(span_f, (META, HD)).astype(BF16)
    v_all[me, 0:HALF], v_all[me, HALF:LD] = ordered(v_ref[...])

    pl.semaphore_wait(barrier, len(peers))

    for give in (send_k, send_v):
        give(me, zdev(1))
        give(me, zdev(-1))
        for dx in OTHERS:
            give(me, xdev(dx))

    for load in loads[3:]:
        load.wait()
    qn[A], qn[B] = ordered(q_ref[...])
    gn[A], gn[B] = ordered(g_ref[...])
    qt[...] = qn[...].T
    gt[...] = gn[...].T
    key_tok = lax.broadcasted_iota(jnp.int32, (HALF, RHALF), 0)
    row_tok = lax.broadcasted_iota(jnp.int32, (HALF, RHALF), 1) // GROUP
    tri = jnp.where(key_tok <= row_tok, 0.0, NEG)
    for rows, keys in ((A, slice(0, HALF)), (B, slice(HALF, LD))):
        s = nn(k_all[me, keys], qt[:, rows]) + tri
        top = col_max(s)
        p = jnp.exp2((s - top) * C2)
        top_s[:, rows] = top
        tot_s[:, rows] = col_sum(p)
        out_s[:, rows] = tn(v_all[me, keys], p.astype(BF16))

    def keys_of(ref, zz, half):
        return ref[pl.ds(zz * NX, NX), half * HALF:(half + 1) * HALF, :].reshape(NX * HALF, HD)

    def bias_of(zz, earlier):
        runs = k_all[pl.ds(zz * NX, NX), LD:, :].astype(F32)[:, 0:8, :]
        seen = (runs < span_f) if earlier else (runs > span_f)
        bias = jnp.where(seen, 0.0, NEG)
        bias = jnp.concatenate([bias] * (RHALF // HD), axis=-1)
        return jnp.broadcast_to(bias[:, None], (NX, HALF // 8, 8, RHALF)).reshape(NX * HALF, RHALF)

    def attend_a(dz):
        zz = zi(dz)
        kl, vl = keys_of(k_all, zz, 0), keys_of(v_all, zz, 0)
        s = nn(kl, qt[:, A]) + bias_of(zz, True)
        old = top_s[:, A]
        top = jnp.maximum(old, col_max(s))
        p = jnp.exp2((s - top) * C2)
        keep = jnp.exp2((old - top) * C2)
        top_s[:, A] = top
        tot_s[:, A] = tot_s[:, A] * keep + col_sum(p)
        out_s[:, A] = out_s[:, A] * keep + tn(vl, p.astype(BF16))

    def attend_b(dz):
        zz = zi(dz)
        kl, ku, vl, vu = (keys_of(r, zz, h) for r in (k_all, v_all) for h in (0, 1))
        s1 = nn(kl, qt[:, B])
        s2 = nn(ku, qt[:, B]) + bias_of(zz, False)
        old = top_s[:, B]
        top = jnp.maximum(old, jnp.maximum(col_max(s1), col_max(s2)))
        p1 = jnp.exp2((s1 - top) * C2)
        p2 = jnp.exp2((s2 - top) * C2)
        keep = jnp.exp2((old - top) * C2)
        top_s[:, B] = top
        tot_s[:, B] = tot_s[:, B] * keep + (col_sum(p1) + col_sum(p2))
        out_s[:, B] = out_s[:, B] * keep + (tn(vl, p1.astype(BF16)) + tn(vu, p2.astype(BF16)))

    def ring(s):
        return [0] if s == 0 else ([far] if s == far else [-s, s])

    def take_k(dz, dx):
        at = slot(dz, dx)
        arrived(k_all.at[at], k_sem.at[at])
        s = abs(dz)
        if s == 0:
            send_k(at, zdev(1))
            send_k(at, zdev(-1))
        elif s + 1 < far or (s + 1 == far and (dx < NX // 2) == (dz < 0)):
            send_k(at, zdev(1 if dz < 0 else -1))

    def take_vz(s):
        for dz in ring(s):
            at = slot(dz, 0)
            arrived(v_all.at[at], v_sem.at[at])
            if s + 1 < far or (s + 1 == far and dz < 0):
                send_v(at, zdev(1 if dz < 0 else -1))
        for dz in ring(s):
            for dx in OTHERS:
                send_v(slot(dz, 0), xdev(dx))

    def take_vx(dz):
        for dx in OTHERS:
            at = slot(dz, dx)
            arrived(v_all.at[at], v_sem.at[at])

    def prepare():
        rw = rw_ref[...].astype(F32)
        rwt[...] = jnp.broadcast_to(rw[None], (LD, GROUP, HD)).reshape(ROWS, HD).T
        row_of = lax.broadcasted_iota(jnp.int32, (ROWS, LD), 0)
        tok_of = lax.broadcasted_iota(jnp.int32, (ROWS, LD), 1)
        to_tok[...] = jnp.where(row_of // GROUP == tok_of, 1.0, 0.0).astype(BF16)
        row_of = lax.broadcasted_iota(jnp.int32, (LD, ROWS), 1)
        tok_of = lax.broadcasted_iota(jnp.int32, (LD, ROWS), 0)
        to_row[...] = jnp.where(row_of // GROUP == tok_of, 1.0, 0.0).astype(BF16)
        s_of = lax.broadcasted_iota(jnp.int32, (STEPS, STEPS), 0)
        t_of = lax.broadcasted_iota(jnp.int32, (STEPS, STEPS), 1)
        lens = jnp.broadcast_to(step_ref[...].astype(F32), (STEPS, STEPS))
        ends = jnp.sum(jnp.where(t_of <= s_of, lens, 0.0), axis=1, keepdims=True) - 1.0
        lane = lax.broadcasted_iota(jnp.int32, (1, LD), 1)
        run = jnp.where(lane < HALF, span_f, (nz * NX * 2 - 1) - span_f)
        tok_pos = run * HALF + (lane % HALF).astype(F32)
        owned_s[...] = jnp.where(ends == tok_pos, 1.0, 0.0)
        dq_s[...] = jnp.zeros(dq_s.shape, F32)

    for s in range(far + 1):
        pieces = []
        if s == 1:
            take_vx(0)
        if s:
            for dz in ring(s - 1):
                pieces += [(attend_a, dz), (attend_b, dz)]
        for i, dx in enumerate((0,) + OTHERS):
            for dz in ring(s):
                if s or dx:
                    take_k(dz, dx)
            if i == 0 and s + 1 <= far:
                take_vz(s + 1)
            if i < len(pieces):
                piece, dz = pieces[i]
                if piece is attend_a and dz:
                    take_vx(dz)
                piece(dz)
        if s == far:
            prepare()
    take_vx(far)
    attend_a(far)
    attend_b(far)

    total = tot_s[...]
    att = (out_s[...] * (1.0 / total)).astype(BF16).astype(F32)
    out_s[...] = att
    lse_s[...] = top_s[...] * C2 + jnp.log2(total)
    def thirds(value):
        one = value.astype(BF16)
        rest = value - one.astype(F32)
        two = rest.astype(BF16)
        return [one, two, (rest - two.astype(F32)).astype(BF16)]

    def rows_of(value):
        pad = jnp.zeros((META - 3,) + value.shape[1:], F32)
        return jnp.concatenate([t.astype(F32) for t in thirds(value)] + [pad], axis=0).astype(BF16)

    score = col_sum(nn(rows_of(col_sum(att * rwt[...])), to_tok[...]))
    hx[hd] = jnp.broadcast_to(score, (8, LD))
    for dh in range(1, nh):
        send(hx.at[hd], hx.at[hd], h_sem.at[hd], hdev(dh))
    early = [far, far - 1, 1 - far, far - 2, 2 - far]

    def blocks(dz):
        zz = zi(dz)
        kl, ku, vl, vu = (keys_of(r, zz, h) for r in (k_all, v_all) for h in (0, 1))
        return ((kl, vl, A, bias_of(zz, True)), (kl, vl, B, None), (ku, vu, B, bias_of(zz, False)))

    def prob_of(k, rows, bias):
        s = nn(k, qt[:, rows])
        if bias is not None:
            s = s + bias
        return jnp.exp2(s * C2 - lse_s[:, rows])

    for j, dz in enumerate(early):
        for b, (k, _, rows, bias) in enumerate(blocks(dz)):
            held[j, b] = prob_of(k, rows, bias)
    owned = owned_s[...]
    owned_low = owned.astype(BF16)
    target = label_ref[...].astype(F32) / ROLLOUTS
    tok_target = nn(jnp.broadcast_to(target, (META, STEPS)).astype(BF16), owned_low)[0:1]
    is_end = col_sum(owned)
    for dh in range(1, nh):
        at = lax.rem(hd + dh, nh)
        arrived(hx.at[at], h_sem.at[at])
    logit = hx[0]
    for h in range(1, nh):
        logit = logit + hx[h]
    logit = logit[0:1]
    misfit = (jax.nn.sigmoid(logit) - tok_target) * is_end
    weight = col_sum(nn(rows_of(misfit), to_row[...]))
    grad = (gt[...].astype(F32) + weight * rwt[...]).astype(BF16)
    gt[...] = grad
    gn[...] = grad.T
    delta_s[...] = col_sum(grad.astype(F32) * att)

    def totals():
        head_of = lax.broadcasted_iota(jnp.int32, (GROUP, ROWS), 0)
        row_of = lax.broadcasted_iota(jnp.int32, (GROUP, ROWS), 1)
        pick = jnp.where(row_of % GROUP == head_of, jnp.broadcast_to(weight, (GROUP, ROWS)), 0.0)
        att_low = out_s[...].astype(BF16)
        parts = [nt(t, att_low) for t in thirds(pick)]
        tx[x, 0:8] = parts[0] + parts[1] + parts[2]
        own = col_sum(nt(rows_of(logit), owned_low))
        tx[x, 8:16] = jnp.broadcast_to(jnp.concatenate([own, jnp.zeros_like(own)], axis=1), (8, LD))
        for dx in OTHERS:
            send(tx.at[x], tx.at[x], tx_sem.at[x], xdev(dx))

    def totals_x():
        for dx in OTHERS:
            at = xi(dx)
            arrived(tx.at[at], tx_sem.at[at])
        tz[z] = tx[0] + tx[1] + tx[2] + tx[3]
        for dz in range(1, nz):
            send(tz.at[z], tz.at[z], tz_sem.at[z], zdev(dz))

    def totals_z():
        for dz in range(1, nz):
            at = zi(dz)
            arrived(tz.at[at], tz_sem.at[at])
        both = tz[0]
        for i in range(1, nz):
            both = both + tz[i]
        dr_ref[...] = both[0:8]
        logits = both[8:9, 0:STEPS]
        soft = jnp.maximum(logits, 0.0) + jnp.log1p(jnp.exp(-jnp.abs(logits)))
        loss_ref[...] = soft - target * logits
        store(dr_ref, dr_hbm)
        store(loss_ref, loss_hbm)

    def back(k, v, rows, p):
        ds = (p * (nn(v, gt[:, rows]) - delta_s[:, rows])).astype(BF16)
        dq_s[:, rows] += tn(k, ds)
        return nn(ds, qn[rows]), nn(p.astype(BF16), gn[rows])

    def back_group(dz):
        (k1, v1), (k2, v2), (k3, v3) = (
            back(k, v, rows, held[early.index(dz), b] if dz in early else prob_of(k, rows, bias))
            for b, (k, v, rows, bias) in enumerate(blocks(dz))
        )
        whole = (NX, HALF, HD)
        return ((k1 + k2) * SCALE).reshape(whole), (k3 * SCALE).reshape(whole), (v1 + v2).reshape(whole), v3.reshape(whole)

    def wide(ref):
        return ref[...].astype(F32)

    FAR, THREE, MID, ONE, OWN = range(5)
    turns = (2,) + tuple(d for d in OTHERS if d != 2) + (0,)

    def comes(level, w, j):
        return level != FAR or (j < NX // 2) == (w == 0)

    def to_owner(level, ways, add=None):
        for j, dx in enumerate(turns):
            for w in ways:
                if not comes(level, w, j):
                    continue
                total = p_k[level, 0 if level == FAR else w, xi(dx)]
                for other in add or ():
                    if comes(other, w, j):
                        total = total + got_k(other, w, j)
                s_k[level, w, j] = total.astype(BF16)
                hops = 2 if level == FAR else 1
                send(s_k.at[level, w, j], r_k.at[level, w, j], rk_sem.at[level, w, j], zdev(-hops if w else hops))

    def got_k(level, w, j):
        arrived(r_k.at[level, w, j], rk_sem.at[level, w, j])
        return wide(r_k.at[level, w, j])

    def give_v(level):
        for dx in OTHERS:
            if level in (FAR, OWN):
                send(p_v.at[level, xi(dx), 0], r_v.at[level, dx, 0], rv_sem.at[level, dx], xdev(dx))
            else:
                send(p_v.at[level, xi(dx)], r_v.at[level, dx], rv_sem.at[level, dx], xdev(dx))

    def sum_v(level):
        one = level in (FAR, OWN)
        total = p_v[level, x, 0].astype(F32) if one else p_v[level, x].astype(F32)
        for dx in OTHERS:
            ref = r_v.at[level, dx, 0] if one else r_v.at[level, dx]
            arrived(ref, rv_sem.at[level, dx])
            total = total + wide(ref)
        return total

    def got_v(level, w):
        arrived(r_v2.at[level, w], vz_sem.at[level, w])
        return wide(r_v2.at[level, w])

    def pass_v(level):
        total = sum_v(level)
        if level == FAR:
            s_v[FAR, 0] = total.astype(BF16)
            send(s_v.at[FAR, 0], r_v2.at[FAR, 0], vz_sem.at[FAR, 0], zdev(2))
            return
        right, left = total[0], total[1]
        if level == MID:
            right = right + got_v(THREE, 0) + got_v(FAR, 0)
            left = left + got_v(THREE, 1)
        if level == ONE:
            right, left = right + got_v(MID, 0), left + got_v(MID, 1)
        for w, value in ((0, right), (1, left)):
            s_v[level, w] = value.astype(BF16)
            send(s_v.at[level, w], r_v2.at[level, w], vz_sem.at[level, w], zdev(-1 if w else 1))

    def group(level, right=True):
        dz = {FAR: far, THREE: 3, MID: 2, ONE: 1, OWN: 0}[level] * (1 if right else -1)
        w = 0 if right else 1
        k_lo, k_hi, v_lo, v_hi = back_group(dz)
        p_v[level, :, w, 0:HALF] = v_lo.astype(BF16)
        p_v[level, :, w, HALF:LD] = v_hi.astype(BF16)
        p_k[level, w, :, 0:HALF], p_k[level, w, :, HALF:LD] = k_lo, k_hi

    group(FAR)
    to_owner(FAR, (0, 1))
    give_v(FAR)
    group(THREE)
    to_owner(THREE, (0,))
    group(THREE, False)
    to_owner(THREE, (1,))
    give_v(THREE)
    group(MID)
    group(MID, False)
    give_v(MID)
    pass_v(FAR)
    to_owner(MID, (0, 1), (THREE, FAR))
    group(ONE)
    totals()
    pass_v(THREE)
    group(ONE, False)
    give_v(ONE)
    to_owner(ONE, (0, 1), (MID,))
    pass_v(MID)
    group(OWN)
    give_v(OWN)
    totals_x()
    for rows, keys in ((A, slice(0, HALF)), (B, slice(HALF, LD))):
        k_own = k_all[me, keys]
        dk_own, dv_own = back(k_own, v_all[me, keys], rows, prob_of(k_own, rows, tri))
        dk_d[keys], dv_d[keys] = dk_own * SCALE, dv_own
    pass_v(ONE)
    for j, dx in enumerate(turns):
        total = p_k[OWN, 0, xi(dx)] + got_k(ONE, 0, j) + got_k(ONE, 1, j)
        if dx:
            s_kx[dx] = total.astype(BF16)
            send(s_kx.at[dx], r_kx.at[dx], kx_sem.at[dx], xdev(dx))
        else:
            dk_d[...] += total
    dq_ref[A], dq_ref[B] = ordered((dq_s[...] * SCALE).T)
    store(dq_ref, dq_hbm)
    dv_d[...] += sum_v(OWN) + got_v(ONE, 0) + got_v(ONE, 1)
    dv_ref[0:HALF], dv_ref[HALF:LD] = ordered(dv_d[...])
    store(dv_ref, dv_hbm)
    totals_z()
    for copy in sends:
        copy.wait_send()
    for dx in OTHERS:
        arrived(r_kx.at[dx], kx_sem.at[dx])
    dk_d[...] += wide(r_kx.at[1]) + wide(r_kx.at[2]) + wide(r_kx.at[3])
    dk_ref[0:HALF], dk_ref[HALF:LD] = ordered(dk_d[...])
    store(dk_ref, dk_hbm)
    for copy in stores:
        copy.wait()


def hand_over(*refs):
    ins, outs, held, (in_sem, out_sem) = refs[:5], refs[5:10], refs[10:15], refs[15:]
    first = [pltpu.make_async_copy(ins[i], held[i], in_sem.at[i]) for i in range(5)]
    second = [pltpu.make_async_copy(held[i], outs[i], out_sem.at[i]) for i in range(5)]
    for copy in first:
        copy.start()
    for one, two in zip(first, second):
        one.wait()
        two.start()
    for copy in second:
        copy.wait()


def local(nz, nh, queries, key_rows, value_rows, token_pos, step_len, label_count, out_grad, reward_weight):
    n = nz * NX
    hbm = pl.BlockSpec(memory_space=pltpu.HBM)
    block = (LD, HD)
    results = [((1, STEPS), F32), ((ROWS, HD), BF16), (block, BF16), (block, BF16), ((GROUP, HD), F32)]
    shapes = [jax.ShapeDtypeStruct(s, t) for s, t in results]
    scratch = results + [
        ((1, LD), jnp.int32), ((1, STEPS), jnp.int32), ((1, STEPS), jnp.int32), ((GROUP, HD), BF16),
        ((ROWS, HD), BF16), ((ROWS, HD), BF16), (block, BF16), (block, BF16),
        ((n, LD + META, HD), BF16), ((n,) + block, BF16),
        ((ROWS, HD), BF16), ((HD, ROWS), BF16), ((ROWS, HD), BF16), ((HD, ROWS), BF16), ((HD, ROWS), F32),
        ((1, ROWS), F32), ((1, ROWS), F32), ((HD, ROWS), F32), ((HD, ROWS), F32), ((1, ROWS), F32), ((1, ROWS), F32),
        ((ROWS, LD), BF16), ((LD, ROWS), BF16), ((STEPS, LD), F32),
        ((nh, 8, HD), F32), ((NX, 16, HD), F32), ((nz, 16, HD), F32),
    ]
    four = (NX,) + block
    scratch += [
        ((5, 3, NX * HALF, RHALF), F32), ((5, 2) + four, F32),
        ((4, 2) + four, BF16), ((4, 2) + four, BF16), (four, BF16), (four, BF16),
        ((5, NX, 2) + block, BF16), ((5, NX, 2) + block, BF16), ((4, 2) + block, BF16), ((4, 2) + block, BF16),
    ]
    scratch += [(block, F32), (block, F32)]
    dma = lambda *shape: pltpu.SemaphoreType.DMA(shape)
    sems = [
        dma(8), dma(5), dma(256), dma(n), dma(n), dma(nh), dma(NX), dma(nz),
        dma(4, 2, NX), dma(NX), dma(5, NX), dma(4, 2),
    ]
    partial = pl.pallas_call(
        functools.partial(kernel, nz, nh),
        out_shape=shapes,
        in_specs=[hbm] * 8,
        out_specs=[hbm] * 5,
        scratch_shapes=[pltpu.VMEM(s, t) for s, t in scratch] + sems,
        compiler_params=pltpu.CompilerParams(
            collective_id=0, has_side_effects=True, vmem_limit_bytes=VMEM_BYTES
        ),
    )(
        token_pos.reshape(1, LD),
        step_len.reshape(1, STEPS),
        label_count.reshape(1, STEPS),
        reward_weight,
        queries.reshape(ROWS, HD),
        out_grad.reshape(ROWS, HD),
        key_rows.reshape(block),
        value_rows.reshape(block),
    )
    loss, dq, dk, dv, dr = pl.pallas_call(
        hand_over,
        out_shape=shapes,
        in_specs=[hbm] * 5,
        out_specs=[hbm] * 5,
        scratch_shapes=[pltpu.VMEM(s, t) for s, t in results] + [dma(5), dma(5)],
        compiler_params=pltpu.CompilerParams(vmem_limit_bytes=VMEM_BYTES),
    )(*partial)
    return (
        loss.reshape(STEPS),
        dq.reshape(queries.shape),
        dk.reshape(key_rows.shape),
        dv.reshape(value_rows.shape),
        dr,
    )


def solution(mesh):
    rows = P(("dp", "ctx"), "head", None)
    return jax.shard_map(
        functools.partial(local, mesh.shape["ctx"] // NX, mesh.shape["head"]),
        mesh=mesh,
        in_specs=(rows, rows, rows, P(("dp", "ctx")), P("dp"), P("dp"), rows, P("head", None)),
        out_specs=(P("dp"), rows, rows, rows, P(("dp", "head"), None)),
        check_vma=False,
    )
```

```python
import functools
import math

import jax
import jax.numpy as jnp
from jax import lax
from jax.experimental import pallas as pl
from jax.experimental.pallas import tpu as pltpu
from jax.sharding import PartitionSpec as P

MESH = pl.DeviceIdType.MESH
F32, BF16 = jnp.float32, jnp.bfloat16
NX = 4
HD = 128
LD = 128
GROUP = 8
HALF = 64
ROWS = LD * GROUP
RHALF = HALF * GROUP
META = 16
STEPS = 64
ROLLOUTS = 8
SCALE = 1.0 / math.sqrt(HD)
LOG2E = math.log2(math.e)
C2 = SCALE * LOG2E
NEG = -1e30
A, B = slice(0, RHALF), slice(RHALF, ROWS)
VMEM_BYTES = 60 * 2**20
PIECES = 4
OTHERS = (1, 3, 2)


def nn(a, b):
    return lax.dot_general(a, b, (((1,), (0,)), ((), ())), preferred_element_type=F32)


def nt(a, b):
    return lax.dot_general(a, b, (((1,), (1,)), ((), ())), preferred_element_type=F32)


def tn(a, b):
    return lax.dot_general(a, b, (((0,), (0,)), ((), ())), preferred_element_type=F32)


def col_max(s):
    return jnp.max(s, axis=0, keepdims=True)


def col_sum(s):
    return jnp.sum(s, axis=0, keepdims=True)


def kernel(
    nz, nh,
    pos_hbm, step_hbm, label_hbm, rw_hbm, q_hbm, g_hbm, k_hbm, v_hbm,
    loss_hbm, dq_hbm, dk_hbm, dv_hbm, dr_hbm,
    loss_ref, dq_ref, dk_ref, dv_ref, dr_ref, pos_ref, step_ref, label_ref, rw_ref, q_ref, g_ref, k_ref, v_ref,
    k_all, v_all, qn, qt, gn, gt, rwt, top_s, tot_s, out_s, dq_s, lse_s, delta_s,
    to_tok, to_row, owned_s, hx, tx, tz,
    held, p_k, s_k, r_k, s_kx, r_kx, p_v, r_v, s_v, r_v2, dk_d, dv_d,
    in_sem, out_sem, send_sem, k_sem, v_sem, h_sem, tx_sem, tz_sem,
    rk_sem, kx_sem, rv_sem, vz_sem,
):
    far = nz // 2
    me = lax.axis_index("ctx")
    hd = lax.axis_index("head")
    z, x = me // NX, me % NX

    def zi(dz):
        return lax.rem(z + (dz + nz), nz)

    def xi(dx):
        return lax.rem(x + (dx + NX), NX)

    def xdev(dx):
        return {"ctx": z * NX + xi(dx)}

    def zdev(dz):
        return {"ctx": zi(dz) * NX + x}

    def hdev(dh):
        return {"head": lax.rem(hd + dh, nh)}

    def slot(dz, dx):
        return zi(dz) * NX + xi(dx)

    sends, stores = [], []

    def store(src, dst):
        copy = pltpu.make_async_copy(src, dst, out_sem.at[len(stores)])
        copy.start()
        stores.append(copy)

    def send(src, dst, recv, dev):
        copy = pltpu.make_async_remote_copy(
            src_ref=src, dst_ref=dst, send_sem=send_sem.at[len(sends)], recv_sem=recv,
            device_id=dev, device_id_type=MESH,
        )
        copy.start()
        sends.append(copy)

    def arrived(dst, recv):
        pltpu.make_async_remote_copy(
            src_ref=dst, dst_ref=dst, send_sem=send_sem.at[0], recv_sem=recv,
            device_id=xdev(1), device_id_type=MESH,
        ).wait_recv()

    def send_k(at, dev):
        send(k_all.at[at], k_all.at[at], k_sem.at[at], dev)

    def send_v(at, dev):
        send(v_all.at[at], v_all.at[at], v_sem.at[at], dev)

    pairs = [
        (pos_hbm, pos_ref), (k_hbm, k_ref), (v_hbm, v_ref), (q_hbm, q_ref), (g_hbm, g_ref),
        (rw_hbm, rw_ref), (step_hbm, step_ref), (label_hbm, label_ref),
    ]
    loads = [pltpu.make_async_copy(src, dst, in_sem.at[i]) for i, (src, dst) in enumerate(pairs)]
    for load in loads[0:3]:
        load.start()

    barrier = pltpu.get_barrier_semaphore()
    peers = [xdev(d) for d in range(1, NX)] + [zdev(d) for d in range(1, nz)] + [hdev(d) for d in range(1, nh)]
    for dev in peers:
        pl.semaphore_signal(barrier, inc=1, device_id=dev, device_id_type=MESH)
    for load in loads[3:]:
        load.start()
    for load in loads[0:3]:
        load.wait()
    pos = pos_ref[...].astype(F32)
    first, second = pos[:, 0:1], pos[:, HALF:HALF + 1]
    span_f = jnp.minimum(first, second) * (1.0 / HALF)
    later_first = jnp.where(first > second, 1.0, 0.0)

    def ordered(value):
        n = value.shape[0] // 2
        one, two = value[:n].astype(F32), value[n:].astype(F32)
        swap = jnp.broadcast_to(later_first, one.shape) > 0.5
        return jnp.where(swap, two, one).astype(BF16), jnp.where(swap, one, two).astype(BF16)

    k_all[me, 0:HALF], k_all[me, HALF:LD] = ordered(k_ref[...])
    k_all[me, LD:] = jnp.broadcast_to(span_f, (META, HD)).astype(BF16)
    v_all[me, 0:HALF], v_all[me, HALF:LD] = ordered(v_ref[...])

    pl.semaphore_wait(barrier, len(peers))

    for give in (send_k, send_v):
        give(me, zdev(1))
        give(me, zdev(-1))
        for dx in OTHERS:
            give(me, xdev(dx))

    for load in loads[3:]:
        load.wait()
    qn[A], qn[B] = ordered(q_ref[...])
    gn[A], gn[B] = ordered(g_ref[...])
    qt[...] = qn[...].T
    gt[...] = gn[...].T
    key_tok = lax.broadcasted_iota(jnp.int32, (HALF, RHALF), 0)
    row_tok = lax.broadcasted_iota(jnp.int32, (HALF, RHALF), 1) // GROUP
    tri = jnp.where(key_tok <= row_tok, 0.0, NEG)
    for rows, keys in ((A, slice(0, HALF)), (B, slice(HALF, LD))):
        s = nn(k_all[me, keys], qt[:, rows]) + tri
        top = col_max(s)
        p = jnp.exp2((s - top) * C2)
        top_s[:, rows] = top
        tot_s[:, rows] = col_sum(p)
        out_s[:, rows] = tn(v_all[me, keys], p.astype(BF16))

    def keys_of(ref, zz, half):
        return ref[pl.ds(zz * NX, NX), half * HALF:(half + 1) * HALF, :].reshape(NX * HALF, HD)

    def bias_of(zz, earlier):
        runs = k_all[pl.ds(zz * NX, NX), LD:, :].astype(F32)[:, 0:8, :]
        seen = (runs < span_f) if earlier else (runs > span_f)
        bias = jnp.where(seen, 0.0, NEG)
        bias = jnp.concatenate([bias] * (RHALF // HD), axis=-1)
        return jnp.broadcast_to(bias[:, None], (NX, HALF // 8, 8, RHALF)).reshape(NX * HALF, RHALF)

    def attend_a(dz):
        zz = zi(dz)
        kl, vl = keys_of(k_all, zz, 0), keys_of(v_all, zz, 0)
        s = nn(kl, qt[:, A]) + bias_of(zz, True)
        old = top_s[:, A]
        top = jnp.maximum(old, col_max(s))
        p = jnp.exp2((s - top) * C2)
        keep = jnp.exp2((old - top) * C2)
        top_s[:, A] = top
        tot_s[:, A] = tot_s[:, A] * keep + col_sum(p)
        out_s[:, A] = out_s[:, A] * keep + tn(vl, p.astype(BF16))

    def attend_b(dz):
        zz = zi(dz)
        kl, ku, vl, vu = (keys_of(r, zz, h) for r in (k_all, v_all) for h in (0, 1))
        s1 = nn(kl, qt[:, B])
        s2 = nn(ku, qt[:, B]) + bias_of(zz, False)
        old = top_s[:, B]
        top = jnp.maximum(old, jnp.maximum(col_max(s1), col_max(s2)))
        p1 = jnp.exp2((s1 - top) * C2)
        p2 = jnp.exp2((s2 - top) * C2)
        keep = jnp.exp2((old - top) * C2)
        top_s[:, B] = top
        tot_s[:, B] = tot_s[:, B] * keep + (col_sum(p1) + col_sum(p2))
        out_s[:, B] = out_s[:, B] * keep + (tn(vl, p1.astype(BF16)) + tn(vu, p2.astype(BF16)))

    def ring(s):
        return [0] if s == 0 else ([far] if s == far else [-s, s])

    def take_k(dz, dx):
        at = slot(dz, dx)
        arrived(k_all.at[at], k_sem.at[at])
        s = abs(dz)
        if s == 0:
            send_k(at, zdev(1))
            send_k(at, zdev(-1))
        elif s + 1 < far or (s + 1 == far and (dx < NX // 2) == (dz < 0)):
            send_k(at, zdev(1 if dz < 0 else -1))

    def take_vz(s):
        for dz in ring(s):
            at = slot(dz, 0)
            arrived(v_all.at[at], v_sem.at[at])
            if s + 1 < far or (s + 1 == far and dz < 0):
                send_v(at, zdev(1 if dz < 0 else -1))
        for dz in ring(s):
            for dx in OTHERS:
                send_v(slot(dz, 0), xdev(dx))

    def take_vx(dz):
        for dx in OTHERS:
            at = slot(dz, dx)
            arrived(v_all.at[at], v_sem.at[at])

    def prepare():
        rw = rw_ref[...].astype(F32)
        rwt[...] = jnp.broadcast_to(rw[None], (LD, GROUP, HD)).reshape(ROWS, HD).T
        row_of = lax.broadcasted_iota(jnp.int32, (ROWS, LD), 0)
        tok_of = lax.broadcasted_iota(jnp.int32, (ROWS, LD), 1)
        to_tok[...] = jnp.where(row_of // GROUP == tok_of, 1.0, 0.0).astype(BF16)
        row_of = lax.broadcasted_iota(jnp.int32, (LD, ROWS), 1)
        tok_of = lax.broadcasted_iota(jnp.int32, (LD, ROWS), 0)
        to_row[...] = jnp.where(row_of // GROUP == tok_of, 1.0, 0.0).astype(BF16)
        s_of = lax.broadcasted_iota(jnp.int32, (STEPS, STEPS), 0)
        t_of = lax.broadcasted_iota(jnp.int32, (STEPS, STEPS), 1)
        lens = jnp.broadcast_to(step_ref[...].astype(F32), (STEPS, STEPS))
        ends = jnp.sum(jnp.where(t_of <= s_of, lens, 0.0), axis=1, keepdims=True) - 1.0
        lane = lax.broadcasted_iota(jnp.int32, (1, LD), 1)
        run = jnp.where(lane < HALF, span_f, (nz * NX * 2 - 1) - span_f)
        tok_pos = run * HALF + (lane % HALF).astype(F32)
        owned_s[...] = jnp.where(ends == tok_pos, 1.0, 0.0)
        dq_s[...] = jnp.zeros(dq_s.shape, F32)

    for s in range(far + 1):
        pieces = []
        if s == 1:
            take_vx(0)
        if s:
            for dz in ring(s - 1):
                pieces += [(attend_a, dz), (attend_b, dz)]
        for i, dx in enumerate((0,) + OTHERS):
            for dz in ring(s):
                if s or dx:
                    take_k(dz, dx)
            if i == 0 and s + 1 <= far:
                take_vz(s + 1)
            if i < len(pieces):
                piece, dz = pieces[i]
                if piece is attend_a and dz:
                    take_vx(dz)
                piece(dz)
        if s == far:
            prepare()
    take_vx(far)
    attend_a(far)
    attend_b(far)

    total = tot_s[...]
    att = (out_s[...] * (1.0 / total)).astype(BF16).astype(F32)
    out_s[...] = att
    lse_s[...] = top_s[...] * C2 + jnp.log2(total)
    def thirds(value):
        one = value.astype(BF16)
        rest = value - one.astype(F32)
        two = rest.astype(BF16)
        return [one, two, (rest - two.astype(F32)).astype(BF16)]

    def rows_of(value):
        pad = jnp.zeros((META - 3,) + value.shape[1:], F32)
        return jnp.concatenate([t.astype(F32) for t in thirds(value)] + [pad], axis=0).astype(BF16)

    score = col_sum(nn(rows_of(col_sum(att * rwt[...])), to_tok[...]))
    hx[hd] = jnp.broadcast_to(score, (8, LD))
    for dh in range(1, nh):
        send(hx.at[hd], hx.at[hd], h_sem.at[hd], hdev(dh))
    early = [far, far - 1, 1 - far, far - 2, 2 - far]

    def blocks(dz):
        zz = zi(dz)
        kl, ku, vl, vu = (keys_of(r, zz, h) for r in (k_all, v_all) for h in (0, 1))
        return ((kl, vl, A, bias_of(zz, True)), (kl, vl, B, None), (ku, vu, B, bias_of(zz, False)))

    def prob_of(k, rows, bias):
        s = nn(k, qt[:, rows])
        if bias is not None:
            s = s + bias
        return jnp.exp2(s * C2 - lse_s[:, rows])

    for j, dz in enumerate(early):
        for b, (k, _, rows, bias) in enumerate(blocks(dz)):
            held[j, b] = prob_of(k, rows, bias)
    owned = owned_s[...]
    owned_low = owned.astype(BF16)
    target = label_ref[...].astype(F32) / ROLLOUTS
    tok_target = nn(jnp.broadcast_to(target, (META, STEPS)).astype(BF16), owned_low)[0:1]
    is_end = col_sum(owned)
    for dh in range(1, nh):
        at = lax.rem(hd + dh, nh)
        arrived(hx.at[at], h_sem.at[at])
    logit = hx[0]
    for h in range(1, nh):
        logit = logit + hx[h]
    logit = logit[0:1]
    misfit = (jax.nn.sigmoid(logit) - tok_target) * is_end
    weight = col_sum(nn(rows_of(misfit), to_row[...]))
    grad = (gt[...].astype(F32) + weight * rwt[...]).astype(BF16)
    gt[...] = grad
    gn[...] = grad.T
    delta_s[...] = col_sum(grad.astype(F32) * att)

    def totals():
        head_of = lax.broadcasted_iota(jnp.int32, (GROUP, ROWS), 0)
        row_of = lax.broadcasted_iota(jnp.int32, (GROUP, ROWS), 1)
        pick = jnp.where(row_of % GROUP == head_of, jnp.broadcast_to(weight, (GROUP, ROWS)), 0.0)
        att_low = out_s[...].astype(BF16)
        parts = [nt(t, att_low) for t in thirds(pick)]
        tx[x, 0:8] = parts[0] + parts[1] + parts[2]
        own = col_sum(nt(rows_of(logit), owned_low))
        tx[x, 8:16] = jnp.broadcast_to(jnp.concatenate([own, jnp.zeros_like(own)], axis=1), (8, LD))
        for dx in OTHERS:
            send(tx.at[x], tx.at[x], tx_sem.at[x], xdev(dx))

    def totals_x():
        for dx in OTHERS:
            at = xi(dx)
            arrived(tx.at[at], tx_sem.at[at])
        tz[z] = tx[0] + tx[1] + tx[2] + tx[3]
        for dz in range(1, nz):
            send(tz.at[z], tz.at[z], tz_sem.at[z], zdev(dz))

    def totals_z():
        for dz in range(1, nz):
            at = zi(dz)
            arrived(tz.at[at], tz_sem.at[at])
        both = tz[0]
        for i in range(1, nz):
            both = both + tz[i]
        dr_ref[...] = both[0:8]
        logits = both[8:9, 0:STEPS]
        soft = jnp.maximum(logits, 0.0) + jnp.log1p(jnp.exp(-jnp.abs(logits)))
        loss_ref[...] = soft - target * logits
        store(dr_ref, dr_hbm)
        store(loss_ref, loss_hbm)

    def back(k, v, rows, p):
        ds = (p * (nn(v, gt[:, rows]) - delta_s[:, rows])).astype(BF16)
        dq_s[:, rows] += tn(k, ds)
        return nn(ds, qn[rows]), nn(p.astype(BF16), gn[rows])

    def back_group(dz):
        (k1, v1), (k2, v2), (k3, v3) = (
            back(k, v, rows, held[early.index(dz), b] if dz in early else prob_of(k, rows, bias))
            for b, (k, v, rows, bias) in enumerate(blocks(dz))
        )
        whole = (NX, HALF, HD)
        return ((k1 + k2) * SCALE).reshape(whole), (k3 * SCALE).reshape(whole), (v1 + v2).reshape(whole), v3.reshape(whole)

    def wide(ref):
        return ref[...].astype(F32)

    FAR, THREE, MID, ONE, OWN = range(5)
    turns = (2,) + tuple(d for d in OTHERS if d != 2) + (0,)

    def comes(level, w, j):
        return level != FAR or (j < NX // 2) == (w == 0)

    def to_owner(level, ways, add=None):
        for j, dx in enumerate(turns):
            for w in ways:
                if not comes(level, w, j):
                    continue
                total = p_k[level, 0 if level == FAR else w, xi(dx)]
                for other in add or ():
                    if comes(other, w, j):
                        total = total + got_k(other, w, j)
                s_k[level, w, j] = total.astype(BF16)
                hops = 2 if level == FAR else 1
                send(s_k.at[level, w, j], r_k.at[level, w, j], rk_sem.at[level, w, j], zdev(-hops if w else hops))

    def got_k(level, w, j):
        arrived(r_k.at[level, w, j], rk_sem.at[level, w, j])
        return wide(r_k.at[level, w, j])

    def give_v(level):
        for dx in OTHERS:
            if level in (FAR, OWN):
                send(p_v.at[level, xi(dx), 0], r_v.at[level, dx, 0], rv_sem.at[level, dx], xdev(dx))
            else:
                send(p_v.at[level, xi(dx)], r_v.at[level, dx], rv_sem.at[level, dx], xdev(dx))

    def sum_v(level):
        one = level in (FAR, OWN)
        total = p_v[level, x, 0].astype(F32) if one else p_v[level, x].astype(F32)
        for dx in OTHERS:
            ref = r_v.at[level, dx, 0] if one else r_v.at[level, dx]
            arrived(ref, rv_sem.at[level, dx])
            total = total + wide(ref)
        return total

    def got_v(level, w, part=slice(0, LD)):
        arrived(r_v2.at[level, w, part], vz_sem.at[level, w])
        return wide(r_v2.at[level, w, part])

    def pass_v(level):
        total = sum_v(level)
        if level == FAR:
            for w, part in ((0, slice(0, HALF)), (1, slice(HALF, LD))):
                s_v[FAR, w, part] = total[part].astype(BF16)
                send(s_v.at[FAR, w, part], r_v2.at[FAR, w, part], vz_sem.at[FAR, w], zdev(-2 if w else 2))
            return
        right, left = total[0], total[1]
        if level == MID:
            right, left = right + got_v(THREE, 0), left + got_v(THREE, 1)
            right = jnp.concatenate([right[:HALF] + got_v(FAR, 0, slice(0, HALF)), right[HALF:]], axis=0)
            left = jnp.concatenate([left[:HALF], left[HALF:] + got_v(FAR, 1, slice(HALF, LD))], axis=0)
        if level == ONE:
            right, left = right + got_v(MID, 0), left + got_v(MID, 1)
        for w, value in ((0, right), (1, left)):
            s_v[level, w] = value.astype(BF16)
            send(s_v.at[level, w], r_v2.at[level, w], vz_sem.at[level, w], zdev(-1 if w else 1))

    def group(level, right=True):
        dz = {FAR: far, THREE: 3, MID: 2, ONE: 1, OWN: 0}[level] * (1 if right else -1)
        w = 0 if right else 1
        k_lo, k_hi, v_lo, v_hi = back_group(dz)
        p_v[level, :, w, 0:HALF] = v_lo.astype(BF16)
        p_v[level, :, w, HALF:LD] = v_hi.astype(BF16)
        p_k[level, w, :, 0:HALF], p_k[level, w, :, HALF:LD] = k_lo, k_hi

    group(FAR)
    to_owner(FAR, (0, 1))
    give_v(FAR)
    group(THREE)
    to_owner(THREE, (0,))
    group(THREE, False)
    to_owner(THREE, (1,))
    give_v(THREE)
    group(MID)
    group(MID, False)
    give_v(MID)
    pass_v(FAR)
    to_owner(MID, (0, 1), (THREE, FAR))
    group(ONE)
    totals()
    pass_v(THREE)
    group(ONE, False)
    give_v(ONE)
    to_owner(ONE, (0, 1), (MID,))
    pass_v(MID)
    group(OWN)
    give_v(OWN)
    totals_x()
    for rows, keys in ((A, slice(0, HALF)), (B, slice(HALF, LD))):
        k_own = k_all[me, keys]
        dk_own, dv_own = back(k_own, v_all[me, keys], rows, prob_of(k_own, rows, tri))
        dk_d[keys], dv_d[keys] = dk_own * SCALE, dv_own
    pass_v(ONE)
    for j, dx in enumerate(turns):
        total = p_k[OWN, 0, xi(dx)] + got_k(ONE, 0, j) + got_k(ONE, 1, j)
        if dx:
            s_kx[dx] = total.astype(BF16)
            send(s_kx.at[dx], r_kx.at[dx], kx_sem.at[dx], xdev(dx))
        else:
            dk_d[...] += total
    dq_ref[A], dq_ref[B] = ordered((dq_s[...] * SCALE).T)
    store(dq_ref, dq_hbm)
    dv_d[...] += sum_v(OWN) + got_v(ONE, 0) + got_v(ONE, 1)
    dv_ref[0:HALF], dv_ref[HALF:LD] = ordered(dv_d[...])
    store(dv_ref, dv_hbm)
    totals_z()
    for copy in sends:
        copy.wait_send()
    for dx in OTHERS:
        arrived(r_kx.at[dx], kx_sem.at[dx])
    dk_d[...] += wide(r_kx.at[1]) + wide(r_kx.at[2]) + wide(r_kx.at[3])
    dk_ref[0:HALF], dk_ref[HALF:LD] = ordered(dk_d[...])
    store(dk_ref, dk_hbm)
    for copy in stores:
        copy.wait()


def hand_over(*refs):
    ins, outs, held, (in_sem, out_sem) = refs[:5], refs[5:10], refs[10:15], refs[15:]
    piece = ROWS // PIECES
    parts = [(1, pl.ds(p * piece, piece)) for p in range(PIECES)] + [(i, slice(None)) for i in (0, 2, 3, 4)]
    first, second = [], []
    for n, (i, at) in enumerate(parts):
        first.append(pltpu.make_async_copy(ins[i].at[at], held[i].at[at], in_sem.at[n]))
        second.append(pltpu.make_async_copy(held[i].at[at], outs[i].at[at], out_sem.at[n]))
    for copy in first:
        copy.start()
    for one, two in zip(first, second):
        one.wait()
        two.start()
    for copy in second:
        copy.wait()


def local(nz, nh, queries, key_rows, value_rows, token_pos, step_len, label_count, out_grad, reward_weight):
    n = nz * NX
    hbm = pl.BlockSpec(memory_space=pltpu.HBM)
    block = (LD, HD)
    results = [((1, STEPS), F32), ((ROWS, HD), BF16), (block, BF16), (block, BF16), ((GROUP, HD), F32)]
    shapes = [jax.ShapeDtypeStruct(s, t) for s, t in results]
    scratch = results + [
        ((1, LD), jnp.int32), ((1, STEPS), jnp.int32), ((1, STEPS), jnp.int32), ((GROUP, HD), BF16),
        ((ROWS, HD), BF16), ((ROWS, HD), BF16), (block, BF16), (block, BF16),
        ((n, LD + META, HD), BF16), ((n,) + block, BF16),
        ((ROWS, HD), BF16), ((HD, ROWS), BF16), ((ROWS, HD), BF16), ((HD, ROWS), BF16), ((HD, ROWS), F32),
        ((1, ROWS), F32), ((1, ROWS), F32), ((HD, ROWS), F32), ((HD, ROWS), F32), ((1, ROWS), F32), ((1, ROWS), F32),
        ((ROWS, LD), BF16), ((LD, ROWS), BF16), ((STEPS, LD), F32),
        ((nh, 8, HD), F32), ((NX, 16, HD), F32), ((nz, 16, HD), F32),
    ]
    four = (NX,) + block
    scratch += [
        ((5, 3, NX * HALF, RHALF), F32), ((5, 2) + four, F32),
        ((4, 2) + four, BF16), ((4, 2) + four, BF16), (four, BF16), (four, BF16),
        ((5, NX, 2) + block, BF16), ((5, NX, 2) + block, BF16), ((4, 2) + block, BF16), ((4, 2) + block, BF16),
    ]
    scratch += [(block, F32), (block, F32)]
    dma = lambda *shape: pltpu.SemaphoreType.DMA(shape)
    sems = [
        dma(8), dma(5), dma(256), dma(n), dma(n), dma(nh), dma(NX), dma(nz),
        dma(4, 2, NX), dma(NX), dma(5, NX), dma(4, 2),
    ]
    partial = pl.pallas_call(
        functools.partial(kernel, nz, nh),
        out_shape=shapes,
        in_specs=[hbm] * 8,
        out_specs=[hbm] * 5,
        scratch_shapes=[pltpu.VMEM(s, t) for s, t in scratch] + sems,
        compiler_params=pltpu.CompilerParams(
            collective_id=0, has_side_effects=True, vmem_limit_bytes=VMEM_BYTES
        ),
    )(
        token_pos.reshape(1, LD),
        step_len.reshape(1, STEPS),
        label_count.reshape(1, STEPS),
        reward_weight,
        queries.reshape(ROWS, HD),
        out_grad.reshape(ROWS, HD),
        key_rows.reshape(block),
        value_rows.reshape(block),
    )
    loss, dq, dk, dv, dr = pl.pallas_call(
        hand_over,
        out_shape=shapes,
        in_specs=[hbm] * 5,
        out_specs=[hbm] * 5,
        scratch_shapes=[pltpu.VMEM(s, t) for s, t in results] + [dma(PIECES + 4), dma(PIECES + 4)],
        compiler_params=pltpu.CompilerParams(vmem_limit_bytes=VMEM_BYTES),
    )(*partial)
    return (
        loss.reshape(STEPS),
        dq.reshape(queries.shape),
        dk.reshape(key_rows.shape),
        dv.reshape(value_rows.shape),
        dr,
    )


def solution(mesh):
    rows = P(("dp", "ctx"), "head", None)
    return jax.shard_map(
        functools.partial(local, mesh.shape["ctx"] // NX, mesh.shape["head"]),
        mesh=mesh,
        in_specs=(rows, rows, rows, P(("dp", "ctx")), P("dp"), P("dp"), rows, P("head", None)),
        out_specs=(P("dp"), rows, rows, rows, P(("dp", "head"), None)),
        check_vma=False,
    )
```

```python
import functools
import math

import jax
import jax.numpy as jnp
from jax import lax
from jax.experimental import pallas as pl
from jax.experimental.pallas import tpu as pltpu
from jax.sharding import PartitionSpec as P

MESH = pl.DeviceIdType.MESH
F32, BF16 = jnp.float32, jnp.bfloat16
NX = 4
HD = 128
LD = 128
GROUP = 8
HALF = 64
ROWS = LD * GROUP
RHALF = HALF * GROUP
META = 16
STEPS = 64
ROLLOUTS = 8
SCALE = 1.0 / math.sqrt(HD)
LOG2E = math.log2(math.e)
C2 = SCALE * LOG2E
NEG = -1e30
A, B = slice(0, RHALF), slice(RHALF, ROWS)
VMEM_BYTES = 60 * 2**20
OTHERS = (2, 1, 3)


def nn(a, b):
    return lax.dot_general(a, b, (((1,), (0,)), ((), ())), preferred_element_type=F32)


def nt(a, b):
    return lax.dot_general(a, b, (((1,), (1,)), ((), ())), preferred_element_type=F32)


def tn(a, b):
    return lax.dot_general(a, b, (((0,), (0,)), ((), ())), preferred_element_type=F32)


def col_max(s):
    return jnp.max(s, axis=0, keepdims=True)


def col_sum(s):
    return jnp.sum(s, axis=0, keepdims=True)


def kernel(
    nz, nh,
    pos_hbm, step_hbm, label_hbm, rw_hbm, q_hbm, g_hbm, k_hbm, v_hbm,
    loss_hbm, dq_hbm, dk_hbm, dv_hbm, dr_hbm,
    loss_ref, dq_ref, dk_ref, dv_ref, dr_ref, pos_ref, step_ref, label_ref, rw_ref, q_ref, g_ref, k_ref, v_ref,
    k_all, v_all, qn, qt, gn, gt, rwt, top_s, tot_s, out_s, dq_s, lse_s, delta_s,
    to_tok, to_row, owned_s, hx, tx, tz,
    held, p_k, s_k, r_k, s_kx, r_kx, p_v, r_v, s_v, r_v2, dk_d, dv_d,
    in_sem, out_sem, send_sem, k_sem, v_sem, h_sem, tx_sem, tz_sem,
    rk_sem, kx_sem, rv_sem, vz_sem,
):
    far = nz // 2
    me = lax.axis_index("ctx")
    hd = lax.axis_index("head")
    z, x = me // NX, me % NX

    def zi(dz):
        return lax.rem(z + (dz + nz), nz)

    def xi(dx):
        return lax.rem(x + (dx + NX), NX)

    def xdev(dx):
        return {"ctx": z * NX + xi(dx)}

    def zdev(dz):
        return {"ctx": zi(dz) * NX + x}

    def hdev(dh):
        return {"head": lax.rem(hd + dh, nh)}

    def slot(dz, dx):
        return zi(dz) * NX + xi(dx)

    sends, stores = [], []

    def store(src, dst):
        copy = pltpu.make_async_copy(src, dst, out_sem.at[len(stores)])
        copy.start()
        stores.append(copy)

    def send(src, dst, recv, dev):
        copy = pltpu.make_async_remote_copy(
            src_ref=src, dst_ref=dst, send_sem=send_sem.at[len(sends)], recv_sem=recv,
            device_id=dev, device_id_type=MESH,
        )
        copy.start()
        sends.append(copy)

    def arrived(dst, recv):
        pltpu.make_async_remote_copy(
            src_ref=dst, dst_ref=dst, send_sem=send_sem.at[0], recv_sem=recv,
            device_id=xdev(1), device_id_type=MESH,
        ).wait_recv()

    def send_k(at, dev):
        send(k_all.at[at], k_all.at[at], k_sem.at[at], dev)

    def send_v(at, dev):
        send(v_all.at[at], v_all.at[at], v_sem.at[at], dev)

    pairs = [
        (pos_hbm, pos_ref), (k_hbm, k_ref), (v_hbm, v_ref), (q_hbm, q_ref), (g_hbm, g_ref),
        (rw_hbm, rw_ref), (step_hbm, step_ref), (label_hbm, label_ref),
    ]
    loads = [pltpu.make_async_copy(src, dst, in_sem.at[i]) for i, (src, dst) in enumerate(pairs)]
    for load in loads[0:3]:
        load.start()

    barrier = pltpu.get_barrier_semaphore()
    peers = [xdev(d) for d in range(1, NX)] + [zdev(d) for d in range(1, nz)] + [hdev(d) for d in range(1, nh)]
    for dev in peers:
        pl.semaphore_signal(barrier, inc=1, device_id=dev, device_id_type=MESH)
    for load in loads[3:]:
        load.start()
    for load in loads[0:3]:
        load.wait()
    pos = pos_ref[...].astype(F32)
    first, second = pos[:, 0:1], pos[:, HALF:HALF + 1]
    span_f = jnp.minimum(first, second) * (1.0 / HALF)
    later_first = jnp.where(first > second, 1.0, 0.0)

    def ordered(value):
        n = value.shape[0] // 2
        one, two = value[:n].astype(F32), value[n:].astype(F32)
        swap = jnp.broadcast_to(later_first, one.shape) > 0.5
        return jnp.where(swap, two, one).astype(BF16), jnp.where(swap, one, two).astype(BF16)

    k_all[me, 0:HALF], k_all[me, HALF:LD] = ordered(k_ref[...])
    k_all[me, LD:] = jnp.broadcast_to(span_f, (META, HD)).astype(BF16)
    v_all[me, 0:HALF], v_all[me, HALF:LD] = ordered(v_ref[...])

    pl.semaphore_wait(barrier, len(peers))

    for give in (send_k, send_v):
        give(me, zdev(1))
        give(me, zdev(-1))
        for dx in OTHERS:
            give(me, xdev(dx))

    for load in loads[3:]:
        load.wait()
    qn[A], qn[B] = ordered(q_ref[...])
    gn[A], gn[B] = ordered(g_ref[...])
    qt[...] = qn[...].T
    gt[...] = gn[...].T
    key_tok = lax.broadcasted_iota(jnp.int32, (HALF, RHALF), 0)
    row_tok = lax.broadcasted_iota(jnp.int32, (HALF, RHALF), 1) // GROUP
    tri = jnp.where(key_tok <= row_tok, 0.0, NEG)
    for rows, keys in ((A, slice(0, HALF)), (B, slice(HALF, LD))):
        s = nn(k_all[me, keys], qt[:, rows]) + tri
        top = col_max(s)
        p = jnp.exp2((s - top) * C2)
        top_s[:, rows] = top
        tot_s[:, rows] = col_sum(p)
        out_s[:, rows] = tn(v_all[me, keys], p.astype(BF16))

    def keys_of(ref, zz, half):
        return ref[pl.ds(zz * NX, NX), half * HALF:(half + 1) * HALF, :].reshape(NX * HALF, HD)

    def bias_of(zz, earlier):
        runs = k_all[pl.ds(zz * NX, NX), LD:, :].astype(F32)[:, 0:8, :]
        seen = (runs < span_f) if earlier else (runs > span_f)
        bias = jnp.where(seen, 0.0, NEG)
        bias = jnp.concatenate([bias] * (RHALF // HD), axis=-1)
        return jnp.broadcast_to(bias[:, None], (NX, HALF // 8, 8, RHALF)).reshape(NX * HALF, RHALF)

    def attend_a(dz):
        zz = zi(dz)
        kl, vl = keys_of(k_all, zz, 0), keys_of(v_all, zz, 0)
        s = nn(kl, qt[:, A]) + bias_of(zz, True)
        old = top_s[:, A]
        top = jnp.maximum(old, col_max(s))
        p = jnp.exp2((s - top) * C2)
        keep = jnp.exp2((old - top) * C2)
        top_s[:, A] = top
        tot_s[:, A] = tot_s[:, A] * keep + col_sum(p)
        out_s[:, A] = out_s[:, A] * keep + tn(vl, p.astype(BF16))

    def attend_b(dz):
        zz = zi(dz)
        kl, ku, vl, vu = (keys_of(r, zz, h) for r in (k_all, v_all) for h in (0, 1))
        s1 = nn(kl, qt[:, B])
        s2 = nn(ku, qt[:, B]) + bias_of(zz, False)
        old = top_s[:, B]
        top = jnp.maximum(old, jnp.maximum(col_max(s1), col_max(s2)))
        p1 = jnp.exp2((s1 - top) * C2)
        p2 = jnp.exp2((s2 - top) * C2)
        keep = jnp.exp2((old - top) * C2)
        top_s[:, B] = top
        tot_s[:, B] = tot_s[:, B] * keep + (col_sum(p1) + col_sum(p2))
        out_s[:, B] = out_s[:, B] * keep + (tn(vl, p1.astype(BF16)) + tn(vu, p2.astype(BF16)))

    def ring(s):
        return [0] if s == 0 else ([far] if s == far else [-s, s])

    def take_k(dz, dx):
        at = slot(dz, dx)
        arrived(k_all.at[at], k_sem.at[at])
        s = abs(dz)
        if s == 0:
            send_k(at, zdev(1))
            send_k(at, zdev(-1))
        elif s + 1 < far or (s + 1 == far and (dx < NX // 2) == (dz < 0)):
            send_k(at, zdev(1 if dz < 0 else -1))

    def take_vz(s):
        for dz in ring(s):
            at = slot(dz, 0)
            arrived(v_all.at[at], v_sem.at[at])
            if s + 1 < far or (s + 1 == far and dz < 0):
                send_v(at, zdev(1 if dz < 0 else -1))
        for dz in ring(s):
            for dx in OTHERS:
                send_v(slot(dz, 0), xdev(dx))

    def take_vx(dz):
        for dx in OTHERS:
            at = slot(dz, dx)
            arrived(v_all.at[at], v_sem.at[at])

    def prepare():
        rw = rw_ref[...].astype(F32)
        rwt[...] = jnp.broadcast_to(rw[None], (LD, GROUP, HD)).reshape(ROWS, HD).T
        row_of = lax.broadcasted_iota(jnp.int32, (ROWS, LD), 0)
        tok_of = lax.broadcasted_iota(jnp.int32, (ROWS, LD), 1)
        to_tok[...] = jnp.where(row_of // GROUP == tok_of, 1.0, 0.0).astype(BF16)
        row_of = lax.broadcasted_iota(jnp.int32, (LD, ROWS), 1)
        tok_of = lax.broadcasted_iota(jnp.int32, (LD, ROWS), 0)
        to_row[...] = jnp.where(row_of // GROUP == tok_of, 1.0, 0.0).astype(BF16)
        s_of = lax.broadcasted_iota(jnp.int32, (STEPS, STEPS), 0)
        t_of = lax.broadcasted_iota(jnp.int32, (STEPS, STEPS), 1)
        lens = jnp.broadcast_to(step_ref[...].astype(F32), (STEPS, STEPS))
        ends = jnp.sum(jnp.where(t_of <= s_of, lens, 0.0), axis=1, keepdims=True) - 1.0
        lane = lax.broadcasted_iota(jnp.int32, (1, LD), 1)
        run = jnp.where(lane < HALF, span_f, (nz * NX * 2 - 1) - span_f)
        tok_pos = run * HALF + (lane % HALF).astype(F32)
        owned_s[...] = jnp.where(ends == tok_pos, 1.0, 0.0)
        dq_s[...] = jnp.zeros(dq_s.shape, F32)

    for s in range(far + 1):
        pieces = []
        if s == 1:
            take_vx(0)
        if s:
            for dz in ring(s - 1):
                pieces += [(attend_a, dz), (attend_b, dz)]
        for i, dx in enumerate((0,) + OTHERS):
            for dz in ring(s):
                if s or dx:
                    take_k(dz, dx)
            if i == 0 and s + 1 <= far:
                take_vz(s + 1)
            if i < len(pieces):
                piece, dz = pieces[i]
                if piece is attend_a and dz:
                    take_vx(dz)
                piece(dz)
        if s == far:
            prepare()
    take_vx(far)
    attend_a(far)
    attend_b(far)

    total = tot_s[...]
    att = (out_s[...] * (1.0 / total)).astype(BF16).astype(F32)
    out_s[...] = att
    lse_s[...] = top_s[...] * C2 + jnp.log2(total)
    def thirds(value):
        one = value.astype(BF16)
        rest = value - one.astype(F32)
        two = rest.astype(BF16)
        return [one, two, (rest - two.astype(F32)).astype(BF16)]

    def rows_of(value):
        pad = jnp.zeros((META - 3,) + value.shape[1:], F32)
        return jnp.concatenate([t.astype(F32) for t in thirds(value)] + [pad], axis=0).astype(BF16)

    score = col_sum(nn(rows_of(col_sum(att * rwt[...])), to_tok[...]))
    hx[hd] = jnp.broadcast_to(score, (8, LD))
    for dh in range(1, nh):
        send(hx.at[hd], hx.at[hd], h_sem.at[hd], hdev(dh))
    early = [far, far - 1, 1 - far, far - 2, 2 - far]

    def blocks(dz):
        zz = zi(dz)
        kl, ku, vl, vu = (keys_of(r, zz, h) for r in (k_all, v_all) for h in (0, 1))
        return ((kl, vl, A, bias_of(zz, True)), (kl, vl, B, None), (ku, vu, B, bias_of(zz, False)))

    def prob_of(k, rows, bias):
        s = nn(k, qt[:, rows])
        if bias is not None:
            s = s + bias
        return jnp.exp2(s * C2 - lse_s[:, rows])

    for j, dz in enumerate(early):
        for b, (k, _, rows, bias) in enumerate(blocks(dz)):
            held[j, b] = prob_of(k, rows, bias)
    owned = owned_s[...]
    owned_low = owned.astype(BF16)
    target = label_ref[...].astype(F32) / ROLLOUTS
    tok_target = nn(jnp.broadcast_to(target, (META, STEPS)).astype(BF16), owned_low)[0:1]
    is_end = col_sum(owned)
    for dh in range(1, nh):
        at = lax.rem(hd + dh, nh)
        arrived(hx.at[at], h_sem.at[at])
    logit = hx[0]
    for h in range(1, nh):
        logit = logit + hx[h]
    logit = logit[0:1]
    misfit = (jax.nn.sigmoid(logit) - tok_target) * is_end
    weight = col_sum(nn(rows_of(misfit), to_row[...]))
    grad = (gt[...].astype(F32) + weight * rwt[...]).astype(BF16)
    gt[...] = grad
    gn[...] = grad.T
    delta_s[...] = col_sum(grad.astype(F32) * att)

    def totals():
        head_of = lax.broadcasted_iota(jnp.int32, (GROUP, ROWS), 0)
        row_of = lax.broadcasted_iota(jnp.int32, (GROUP, ROWS), 1)
        pick = jnp.where(row_of % GROUP == head_of, jnp.broadcast_to(weight, (GROUP, ROWS)), 0.0)
        att_low = out_s[...].astype(BF16)
        parts = [nt(t, att_low) for t in thirds(pick)]
        tx[x, 0:8] = parts[0] + parts[1] + parts[2]
        own = col_sum(nt(rows_of(logit), owned_low))
        tx[x, 8:16] = jnp.broadcast_to(jnp.concatenate([own, jnp.zeros_like(own)], axis=1), (8, LD))
        for dx in OTHERS:
            send(tx.at[x], tx.at[x], tx_sem.at[x], xdev(dx))

    def totals_x():
        for dx in OTHERS:
            at = xi(dx)
            arrived(tx.at[at], tx_sem.at[at])
        tz[z] = tx[0] + tx[1] + tx[2] + tx[3]
        for dz in range(1, nz):
            send(tz.at[z], tz.at[z], tz_sem.at[z], zdev(dz))

    def totals_z():
        for dz in range(1, nz):
            at = zi(dz)
            arrived(tz.at[at], tz_sem.at[at])
        both = tz[0]
        for i in range(1, nz):
            both = both + tz[i]
        dr_ref[...] = both[0:8]
        logits = both[8:9, 0:STEPS]
        soft = jnp.maximum(logits, 0.0) + jnp.log1p(jnp.exp(-jnp.abs(logits)))
        loss_ref[...] = soft - target * logits
        store(dr_ref, dr_hbm)
        store(loss_ref, loss_hbm)

    def back(k, v, rows, p):
        ds = (p * (nn(v, gt[:, rows]) - delta_s[:, rows])).astype(BF16)
        dq_s[:, rows] += tn(k, ds)
        return nn(ds, qn[rows]), nn(p.astype(BF16), gn[rows])

    def back_group(dz):
        (k1, v1), (k2, v2), (k3, v3) = (
            back(k, v, rows, held[early.index(dz), b] if dz in early else prob_of(k, rows, bias))
            for b, (k, v, rows, bias) in enumerate(blocks(dz))
        )
        whole = (NX, HALF, HD)
        return ((k1 + k2) * SCALE).reshape(whole), (k3 * SCALE).reshape(whole), (v1 + v2).reshape(whole), v3.reshape(whole)

    def wide(ref):
        return ref[...].astype(F32)

    FAR, THREE, MID, ONE, OWN = range(5)
    turns = (2,) + tuple(d for d in OTHERS if d != 2) + (0,)

    def comes(level, w, j):
        return level != FAR or (j < NX // 2) == (w == 0)

    def to_owner(level, ways, add=None):
        for j, dx in enumerate(turns):
            for w in ways:
                if not comes(level, w, j):
                    continue
                total = p_k[level, 0 if level == FAR else w, xi(dx)]
                for other in add or ():
                    if comes(other, w, j):
                        total = total + got_k(other, w, j)
                s_k[level, w, j] = total.astype(BF16)
                hops = 2 if level == FAR else 1
                send(s_k.at[level, w, j], r_k.at[level, w, j], rk_sem.at[level, w, j], zdev(-hops if w else hops))

    def got_k(level, w, j):
        arrived(r_k.at[level, w, j], rk_sem.at[level, w, j])
        return wide(r_k.at[level, w, j])

    def give_v(level):
        for dx in OTHERS:
            if level in (FAR, OWN):
                send(p_v.at[level, xi(dx), 0], r_v.at[level, dx, 0], rv_sem.at[level, dx], xdev(dx))
            else:
                send(p_v.at[level, xi(dx)], r_v.at[level, dx], rv_sem.at[level, dx], xdev(dx))

    def sum_v(level):
        one = level in (FAR, OWN)
        total = p_v[level, x, 0].astype(F32) if one else p_v[level, x].astype(F32)
        for dx in OTHERS:
            ref = r_v.at[level, dx, 0] if one else r_v.at[level, dx]
            arrived(ref, rv_sem.at[level, dx])
            total = total + wide(ref)
        return total

    def got_v(level, w):
        arrived(r_v2.at[level, w], vz_sem.at[level, w])
        return wide(r_v2.at[level, w])

    def pass_v(level):
        total = sum_v(level)
        if level == FAR:
            s_v[FAR, 0] = total.astype(BF16)
            send(s_v.at[FAR, 0], r_v2.at[FAR, 0], vz_sem.at[FAR, 0], zdev(2))
            return
        right, left = total[0], total[1]
        if level == MID:
            right = right + got_v(THREE, 0) + got_v(FAR, 0)
            left = left + got_v(THREE, 1)
        if level == ONE:
            right, left = right + got_v(MID, 0), left + got_v(MID, 1)
        for w, value in ((0, right), (1, left)):
            s_v[level, w] = value.astype(BF16)
            send(s_v.at[level, w], r_v2.at[level, w], vz_sem.at[level, w], zdev(-1 if w else 1))

    def group(level, right=True):
        dz = {FAR: far, THREE: 3, MID: 2, ONE: 1, OWN: 0}[level] * (1 if right else -1)
        w = 0 if right else 1
        k_lo, k_hi, v_lo, v_hi = back_group(dz)
        p_v[level, :, w, 0:HALF] = v_lo.astype(BF16)
        p_v[level, :, w, HALF:LD] = v_hi.astype(BF16)
        p_k[level, w, :, 0:HALF], p_k[level, w, :, HALF:LD] = k_lo, k_hi

    group(FAR)
    to_owner(FAR, (0, 1))
    give_v(FAR)
    group(THREE)
    to_owner(THREE, (0,))
    group(THREE, False)
    to_owner(THREE, (1,))
    give_v(THREE)
    group(MID)
    group(MID, False)
    give_v(MID)
    pass_v(FAR)
    to_owner(MID, (0, 1), (THREE, FAR))
    group(ONE)
    totals()
    pass_v(THREE)
    group(ONE, False)
    give_v(ONE)
    to_owner(ONE, (0, 1), (MID,))
    pass_v(MID)
    group(OWN)
    give_v(OWN)
    totals_x()
    for rows, keys in ((A, slice(0, HALF)), (B, slice(HALF, LD))):
        k_own = k_all[me, keys]
        dk_own, dv_own = back(k_own, v_all[me, keys], rows, prob_of(k_own, rows, tri))
        dk_d[keys], dv_d[keys] = dk_own * SCALE, dv_own
    pass_v(ONE)
    for j, dx in enumerate(turns):
        total = p_k[OWN, 0, xi(dx)] + got_k(ONE, 0, j) + got_k(ONE, 1, j)
        if dx:
            s_kx[dx] = total.astype(BF16)
            send(s_kx.at[dx], r_kx.at[dx], kx_sem.at[dx], xdev(dx))
        else:
            dk_d[...] += total
    dq_ref[A], dq_ref[B] = ordered((dq_s[...] * SCALE).T)
    store(dq_ref, dq_hbm)
    dv_d[...] += sum_v(OWN) + got_v(ONE, 0) + got_v(ONE, 1)
    dv_ref[0:HALF], dv_ref[HALF:LD] = ordered(dv_d[...])
    store(dv_ref, dv_hbm)
    totals_z()
    for copy in sends:
        copy.wait_send()
    for dx in OTHERS:
        arrived(r_kx.at[dx], kx_sem.at[dx])
    dk_d[...] += wide(r_kx.at[1]) + wide(r_kx.at[2]) + wide(r_kx.at[3])
    dk_ref[0:HALF], dk_ref[HALF:LD] = ordered(dk_d[...])
    store(dk_ref, dk_hbm)
    for copy in stores:
        copy.wait()


def hand_over(*refs):
    ins, outs, held, (in_sem, out_sem) = refs[:5], refs[5:10], refs[10:15], refs[15:]
    first = [pltpu.make_async_copy(ins[i], held[i], in_sem.at[i]) for i in range(5)]
    second = [pltpu.make_async_copy(held[i], outs[i], out_sem.at[i]) for i in range(5)]
    for copy in first:
        copy.start()
    for one, two in zip(first, second):
        one.wait()
        two.start()
    for copy in second:
        copy.wait()


def local(nz, nh, queries, key_rows, value_rows, token_pos, step_len, label_count, out_grad, reward_weight):
    n = nz * NX
    hbm = pl.BlockSpec(memory_space=pltpu.HBM)
    block = (LD, HD)
    results = [((1, STEPS), F32), ((ROWS, HD), BF16), (block, BF16), (block, BF16), ((GROUP, HD), F32)]
    shapes = [jax.ShapeDtypeStruct(s, t) for s, t in results]
    scratch = results + [
        ((1, LD), jnp.int32), ((1, STEPS), jnp.int32), ((1, STEPS), jnp.int32), ((GROUP, HD), BF16),
        ((ROWS, HD), BF16), ((ROWS, HD), BF16), (block, BF16), (block, BF16),
        ((n, LD + META, HD), BF16), ((n,) + block, BF16),
        ((ROWS, HD), BF16), ((HD, ROWS), BF16), ((ROWS, HD), BF16), ((HD, ROWS), BF16), ((HD, ROWS), F32),
        ((1, ROWS), F32), ((1, ROWS), F32), ((HD, ROWS), F32), ((HD, ROWS), F32), ((1, ROWS), F32), ((1, ROWS), F32),
        ((ROWS, LD), BF16), ((LD, ROWS), BF16), ((STEPS, LD), F32),
        ((nh, 8, HD), F32), ((NX, 16, HD), F32), ((nz, 16, HD), F32),
    ]
    four = (NX,) + block
    scratch += [
        ((5, 3, NX * HALF, RHALF), F32), ((5, 2) + four, F32),
        ((4, 2) + four, BF16), ((4, 2) + four, BF16), (four, BF16), (four, BF16),
        ((5, NX, 2) + block, BF16), ((5, NX, 2) + block, BF16), ((4, 2) + block, BF16), ((4, 2) + block, BF16),
    ]
    scratch += [(block, F32), (block, F32)]
    dma = lambda *shape: pltpu.SemaphoreType.DMA(shape)
    sems = [
        dma(8), dma(5), dma(256), dma(n), dma(n), dma(nh), dma(NX), dma(nz),
        dma(4, 2, NX), dma(NX), dma(5, NX), dma(4, 2),
    ]
    partial = pl.pallas_call(
        functools.partial(kernel, nz, nh),
        out_shape=shapes,
        in_specs=[hbm] * 8,
        out_specs=[hbm] * 5,
        scratch_shapes=[pltpu.VMEM(s, t) for s, t in scratch] + sems,
        compiler_params=pltpu.CompilerParams(
            collective_id=0, has_side_effects=True, vmem_limit_bytes=VMEM_BYTES
        ),
    )(
        token_pos.reshape(1, LD),
        step_len.reshape(1, STEPS),
        label_count.reshape(1, STEPS),
        reward_weight,
        queries.reshape(ROWS, HD),
        out_grad.reshape(ROWS, HD),
        key_rows.reshape(block),
        value_rows.reshape(block),
    )
    loss, dq, dk, dv, dr = pl.pallas_call(
        hand_over,
        out_shape=shapes,
        in_specs=[hbm] * 5,
        out_specs=[hbm] * 5,
        scratch_shapes=[pltpu.VMEM(s, t) for s, t in results] + [dma(5), dma(5)],
        compiler_params=pltpu.CompilerParams(vmem_limit_bytes=VMEM_BYTES),
    )(*partial)
    return (
        loss.reshape(STEPS),
        dq.reshape(queries.shape),
        dk.reshape(key_rows.shape),
        dv.reshape(value_rows.shape),
        dr,
    )


def solution(mesh):
    rows = P(("dp", "ctx"), "head", None)
    return jax.shard_map(
        functools.partial(local, mesh.shape["ctx"] // NX, mesh.shape["head"]),
        mesh=mesh,
        in_specs=(rows, rows, rows, P(("dp", "ctx")), P("dp"), P("dp"), rows, P("head", None)),
        out_specs=(P("dp"), rows, rows, rows, P(("dp", "head"), None)),
        check_vma=False,
    )
```
